768 devices in a mesh: row: 16 (over x_hi, y), col: 48 (over x_lo, z, core).
Axes of the slice: x: 4 (x_hi: 2, x_lo: 2; x = x_hi * 2 + x_lo), y: 8, z: 12, core: 2. Of those that a mesh axis runs over, the one named last changes fastest.
Arguments:
- density: float32 [6144, 6144], P('row', 'col'), as said below
- atom_sizes: int32 [96], replicated, may hold values from 32 to 64
- pattern: int32 [96, 96], P('row', 'col'), may hold values from 0 to 1, as said below
- kept: int32 [96, 96], P('row', 'col'), may hold values 0 or 1
Outputs:
- square: float32 [6144, 6144], P('row', 'col')
- purified: float32 [6144, 6144], P('row', 'col')
The draws below stay inside these ranges and needn't reach their ends.
Inputs may be any that keep to these rules, and one draw needn't show every extreme that they name: density is symmetric. pattern is symmetric.
All inputs are finite; a program needn't handle non-finite values. No bound on the sum of `kept` on one device may be relied on, other than what follows from the above.
Results may differ from the reference program's by a relative error of at most 0.000059.
Values sent between devices are 32-bit elements; how exact they have to be, the bound alone decides.
No kernel may reach another device: no remote copies, remote signals or barrier semaphores. Data moves between devices by JAX's collectives and lax.ppermute only.
A program may use at most 32 MiB of HBM per device.

```python
import jax
import jax.numpy as jnp
from jax import lax

NB = 96
BS = 64


def draw_density(key, part):
    key = jax.random.fold_in(key, 11)
    scale = (NB * BS) ** (-0.25)
    values = jax.random.normal(key, (NB * BS, NB * BS), jnp.float32)
    return (values + values.T) * (0.70710678 * scale)


def draw_pattern(key, part):
    key = jax.random.fold_in(key, 23)
    upper = jax.random.randint(key, (NB, NB), 0, 2).astype(jnp.int32)
    rows = jnp.arange(NB, dtype=jnp.int32)[:, None]
    cols = jnp.arange(NB, dtype=jnp.int32)[None, :]
    return jnp.where(rows <= cols, upper, upper.T)


def place_ends(entries, own_key, least, top_value):
    dims = entries.shape
    index_at = [jax.random.randint(jax.random.fold_in(own_key, axis), (), 0, dims[axis]) for axis in range(len(dims))]
    entries = entries.at[tuple(index_at)].set(least)
    longest = dims.index(max(dims))
    index_at[longest] = (index_at[longest] + 1) % dims[longest]
    return entries.at[tuple(index_at)].set(top_value)


def setup_inputs(seed: int = 0) -> dict:
    arg_keys = jax.random.split(jax.random.key(seed), 5)
    density = draw_density(jax.random.fold_in(arg_keys[4], 71), 0)
    atom_sizes = place_ends(jax.random.randint(arg_keys[1], (NB,), BS // 2, BS + 1), jax.random.fold_in(arg_keys[1], 1), BS // 2, BS).astype(jnp.int32)
    pattern = draw_pattern(jax.random.fold_in(arg_keys[4], 71), 0)
    kept = place_ends((jax.random.randint(arg_keys[3], (NB, NB), 0, 4) < 3).astype(jnp.int32), jax.random.fold_in(arg_keys[3], 1), 0, 1)
    return dict(density=density, atom_sizes=atom_sizes, pattern=pattern, kept=kept)


def build_mask(atom_sizes, pattern, kept):
    offsets = jnp.arange(BS, dtype=jnp.int32)
    valid = (offsets[None, :] < atom_sizes[:, None]).astype(jnp.float32)
    patf = pattern.astype(jnp.float32)
    mask = patf[:, None, :, None] * valid[:, :, None, None] * valid[None, None, :, :]
    filt = jnp.broadcast_to(kept.astype(jnp.float32)[:, None, :, None], (NB, BS, NB, BS))
    return mask.reshape(NB * BS, NB * BS), filt.reshape(NB * BS, NB * BS)


def reference(density, atom_sizes, pattern, kept):
    mask, filt = build_mask(atom_sizes, pattern, kept)
    masked = density * mask
    square = filt * jnp.dot(masked, masked, precision=lax.Precision.HIGHEST, preferred_element_type=jnp.float32)
    cube = filt * jnp.dot(square, masked, precision=lax.Precision.HIGHEST, preferred_element_type=jnp.float32)
    purified = 3.0 * square - 2.0 * cube
    return square, purified
```

```python
import jax
import jax.numpy as jnp
from jax import lax
from jax.sharding import Mesh, PartitionSpec as P

BS = 64
AXES = ("xh", "y", "xl", "z", "c")
ROW = ("xh", "y")
COL = ("xl", "z", "c")


def local_masks(atom_sizes, pattern, kept):
    row_blocks, col_blocks = pattern.shape
    first_row = lax.axis_index(ROW) * row_blocks
    first_col = lax.axis_index(COL) * col_blocks
    offsets = jnp.arange(BS, dtype=jnp.int32)
    sizes_rows = lax.dynamic_slice_in_dim(atom_sizes, first_row, row_blocks, 0)
    sizes_cols = lax.dynamic_slice_in_dim(atom_sizes, first_col, col_blocks, 0)
    valid_rows = (offsets[None, :] < sizes_rows[:, None]).astype(jnp.float32)
    valid_cols = (offsets[None, :] < sizes_cols[:, None]).astype(jnp.float32)
    patf = pattern.astype(jnp.float32)
    mask = patf[:, None, :, None] * valid_rows[:, :, None, None] * valid_cols[None, None, :, :]
    filt = jnp.broadcast_to(
        kept.astype(jnp.float32)[:, None, :, None], (row_blocks, BS, col_blocks, BS)
    )
    shape = (row_blocks * BS, col_blocks * BS)
    return (mask.reshape(shape), filt.reshape(shape))


def body(density, atom_sizes, pattern, kept):
    mask, filt = local_masks(atom_sizes, pattern, kept)
    masked = density * mask
    rows, cols = masked.shape
    xl = lax.axis_index("xl")

    left = lax.all_gather(masked, ("z", "c"), axis=1, tiled=True)

    four = lax.all_gather(masked, ("xh", "xl"), axis=0)
    four = four.reshape(2, 2, rows, cols)
    pair = lax.dynamic_index_in_dim(four, xl, 0, keepdims=False)
    pair = jnp.concatenate([pair[0], pair[1]], axis=1)
    right = lax.all_gather(pair, "y", axis=0, tiled=True)

    def product(a):
        part = jnp.dot(
            a, right, precision=lax.Precision.HIGHEST, preferred_element_type=jnp.float32
        )
        part = jnp.stack([part[:, :cols], part[:, cols:]])
        mine = lax.dynamic_index_in_dim(part, xl, 0, keepdims=False)
        other = lax.dynamic_index_in_dim(part, 1 - xl, 0, keepdims=False)
        return mine + lax.ppermute(other, "xl", [(0, 1), (1, 0)])

    square = filt * product(left)
    cube = filt * product(lax.all_gather(square, ("z", "c"), axis=1, tiled=True))
    purified = 3.0 * square - 2.0 * cube
    return (square, purified)


def solution(mesh):
    fine = Mesh(mesh.devices.reshape(2, 8, 2, 12, 2), AXES)
    placed = (P(ROW, COL), P(), P(ROW, COL), P(ROW, COL))
    return jax.shard_map(
        body,
        mesh=fine,
        in_specs=placed,
        out_specs=(P(ROW, COL), P(ROW, COL)),
        check_vma=False,
    )
```

```python
import functools

import jax
import jax.numpy as jnp
from jax import lax
from jax.experimental import pallas as pl
from jax.experimental.pallas import tpu as pltpu
from jax.sharding import Mesh, PartitionSpec as P

BS = 64
AXES = ("xh", "y", "xl", "z", "c")
SIZES = (2, 8, 2, 12, 2)
NY = 8
NZ = 12
ROW = ("xh", "y")
COL = ("xl", "z", "c")
F32 = jnp.float32
BF16 = jnp.bfloat16
VM = pl.BlockSpec(memory_space=pltpu.VMEM)
SM = pl.BlockSpec(memory_space=pltpu.SMEM)
PARAMS = pltpu.CompilerParams(vmem_limit_bytes=32 * 1024 * 1024)


def mask_kernel(sizes, pattern, density, out):
    row_blocks, col_blocks = pattern.shape
    first_row = (lax.axis_index("xh") * NY + lax.axis_index("y")) * row_blocks
    first_col = ((lax.axis_index("xl") * NZ + lax.axis_index("z")) * 2 + lax.axis_index("c")) * col_blocks
    sub = lax.broadcasted_iota(jnp.int32, (BS, 2 * BS), 0)
    lane = lax.broadcasted_iota(jnp.int32, (BS, 2 * BS), 1)
    left = lane < BS
    size_col = jnp.where(left, sizes[first_col], sizes[first_col + 1])
    valid_col = (jnp.where(left, lane, lane - BS) < size_col).astype(F32)
    for i in range(row_blocks):
        stored = jnp.where(left, pattern[i, 0], pattern[i, 1]).astype(F32)
        valid = (sub < sizes[first_row + i]).astype(F32) * valid_col * stored
        out[i * BS : (i + 1) * BS, :] = density[i * BS : (i + 1) * BS, :] * valid


def split(x):
    hi = x.astype(BF16)
    return hi, (x - hi.astype(F32)).astype(BF16)


def product_kernel(plan, has_acc, last, *refs):
    n_in = 1 + sum(1 if kind == "both" else 2 for kind, _ in plan)
    right = refs[0]
    acc = refs[n_in][...] if has_acc else None
    outs = refs[n_in + has_acc :]
    z = lax.axis_index("z")
    c = lax.axis_index("c")

    def unit(u):
        y = u // 3
        rows = pl.ds(pl.multiple_of((u - 3 * y) * 128, 128), 128)
        return jnp.concatenate([right[y, 0, rows, :], right[y, 1, rows, :]], axis=1)

    dot = functools.partial(jnp.dot, preferred_element_type=F32)
    at = 1
    for kind, offsets in plan:
        for k, off in enumerate(offsets):
            zz = lax.rem(z + (off + NZ), NZ)
            if kind == "both":
                a = jnp.concatenate([refs[at][0], refs[at][1]], axis=1)
                first, second = 2 * zz, 2 * zz + 1
            else:
                a = jnp.concatenate([refs[at][k], refs[at + 1][k]], axis=1)
                first, second = 2 * zz + c, 2 * zz + 1 - c
            b = jnp.concatenate([unit(first), unit(second)], axis=0)
            ah, al = split(a)
            bh, bl = split(b)
            term = dot(ah, bh) + (dot(ah, bl) + dot(al, bh))
            acc = term if acc is None else acc + term
        at += 1 if kind == "both" else 2
    if not last:
        outs[0][...] = acc
        return
    same = lax.axis_index("xl") == lax.axis_index("xh")
    near, far = acc[:, :128], acc[:, 128:]
    outs[0][...] = jnp.where(same, near, far)
    outs[1][...] = jnp.where(same, far, near)


def product(right, groups, acc=None, last=True):
    plan = tuple((kind, offsets) for kind, offsets, _ in groups)
    n = sum(len(offsets) for _, offsets in plan)
    rows, cols = groups[0][2][0].shape[1:]
    args = [right] + [x for _, _, arrays in groups for x in arrays]
    if acc is not None:
        args.append(acc)
    if last:
        shapes = (jax.ShapeDtypeStruct((rows, cols), F32),) * 2
    else:
        shapes = jax.ShapeDtypeStruct((rows, 2 * cols), F32)
    return pl.pallas_call(
        functools.partial(product_kernel, plan, acc is not None, last),
        out_shape=shapes,
        in_specs=[VM] * len(args),
        out_specs=(VM, VM) if last else VM,
        compiler_params=PARAMS,
        cost_estimate=pl.CostEstimate(
            flops=n * 3 * 2 * rows * 2 * cols * 2 * cols, bytes_accessed=0, transcendentals=0
        ),
    )(*args)


def filter_kernel(final, kept, mine, pair, *refs):
    other = 1 - lax.axis_index("xl")
    lane = lax.broadcasted_iota(jnp.int32, (BS, 2 * BS), 1)
    for i in range(kept.shape[0]):
        strip = slice(i * BS, (i + 1) * BS)
        filt = jnp.where(lane < BS, kept[i, 0], kept[i, 1]).astype(F32)
        total = filt * (mine[strip, :] + pair[other, strip, :])
        if final:
            refs[1][strip, :] = 3.0 * refs[0][strip, :] - 2.0 * total
        else:
            refs[0][strip, :] = total


def filtered(kept, halves, square=None):
    mine, other = halves
    pair = lax.all_gather(other, "xl", axis=0)
    args = [kept, mine, pair] + ([] if square is None else [square])
    return pl.pallas_call(
        functools.partial(filter_kernel, square is not None),
        out_shape=jax.ShapeDtypeStruct(mine.shape, F32),
        in_specs=[SM] + [VM] * (len(args) - 1),
        out_specs=VM,
        compiler_params=PARAMS,
    )(*args)


def shift(x, axis, step):
    n = SIZES[AXES.index(axis)]
    return lax.ppermute(x, axis, [(i, (i + step) % n) for i in range(n)])


def together(*xs):
    return lax.optimization_barrier(xs)


def body(density, atom_sizes, pattern, kept):
    masked = pl.pallas_call(
        mask_kernel,
        out_shape=jax.ShapeDtypeStruct(density.shape, F32),
        in_specs=[SM, SM, VM],
        out_specs=VM,
        compiler_params=PARAMS,
    )(atom_sizes, pattern, density)

    near = lax.ppermute(masked, ("xh", "xl"), [(0, 0), (1, 2), (2, 1), (3, 3)])
    far = lax.ppermute(masked, ("xh", "xl"), [(1, 0), (2, 3), (0, 2), (3, 1)])
    up, down = shift(masked, "z", 1), shift(masked, "z", -1)
    u1, d1, near, far = together(up, down, near, far)
    right, u1, d1 = together(jnp.stack([near, far]), u1, d1)
    right = lax.all_gather(right, "y", axis=0)

    def rest(x, u1, d1, multiply, alone):
        x = x[None]
        u2, d2, x_sib = together(shift(u1, "z", 1), shift(d1, "z", -1), shift(x, "c", 1))
        s12 = jnp.stack([u1, d1, u2, d2])
        u3, d3, s12_sib = together(shift(u2, "z", 1), shift(d2, "z", -1), shift(s12, "c", 1))
        g12 = [("pair", (0,), (x, x_sib)), ("pair", (-1, 1, -2, 2), (s12, s12_sib))]
        acc = multiply(g12)
        u4, d4, acc = together(shift(u3, "z", 1), shift(d3, "z", -1), acc)
        s34 = jnp.stack([u3, d3, u4, d4])
        u5, d5, s34_sib = together(shift(u4, "z", 1), shift(d4, "z", -1), shift(s34, "c", 1))
        g34 = [("pair", (-3, 3, -4, 4), (s34, s34_sib))]
        acc = multiply(g34, acc)
        s5 = jnp.stack([u5, d5])
        u6, s5_sib, acc = together(shift(u5, "z", 1), shift(s5, "c", 1), acc)
        g56 = [("pair", (-5, 5), (s5, s5_sib))]
        if alone:
            g56.append(("both", (-6,), (lax.all_gather(u6, "c", axis=0),)))
        else:
            g56.append(("pair", (-6,), (u6[None], shift(u6[None], "c", 1))))
        return g12 + g34, g56, acc

    def later(groups, acc=None):
        return jnp.zeros((), F32) if acc is None else acc

    def now(groups, acc=None):
        return product(right, groups, acc, last=False)

    most, final, _ = rest(masked, u1, d1, later, False)
    square = filtered(kept, product(right, most + final))

    u1, d1 = together(shift(square, "z", 1), shift(square, "z", -1))
    _, final, acc = rest(square, u1, d1, now, True)
    purified = filtered(kept, product(right, final, acc), square)
    return (square, purified)


def solution(mesh):
    fine = Mesh(mesh.devices.reshape(SIZES), AXES)
    placed = (P(ROW, COL), P(), P(ROW, COL), P(ROW, COL))
    return jax.shard_map(
        body,
        mesh=fine,
        in_specs=placed,
        out_specs=(P(ROW, COL), P(ROW, COL)),
        check_vma=False,
    )
```

```python
import functools

import jax
import jax.numpy as jnp
from jax import lax
from jax.experimental import pallas as pl
from jax.experimental.pallas import tpu as pltpu
from jax.sharding import Mesh, PartitionSpec as P

BS = 64
AXES = ("xh", "y", "xl", "z", "c")
SIZES = (2, 8, 2, 12, 2)
NY = 8
NZ = 12
ROW = ("xh", "y")
COL = ("xl", "z", "c")
F32 = jnp.float32
BF16 = jnp.bfloat16
VM = pl.BlockSpec(memory_space=pltpu.VMEM)
SM = pl.BlockSpec(memory_space=pltpu.SMEM)
PARAMS = pltpu.CompilerParams(vmem_limit_bytes=32 * 1024 * 1024)


def mask_kernel(sizes, pattern, density, out):
    col_blocks, row_blocks = pattern.shape
    first_row = (lax.axis_index("xh") * NY + lax.axis_index("y")) * row_blocks
    first_col = ((lax.axis_index("xl") * NZ + lax.axis_index("z")) * 2 + lax.axis_index("c")) * col_blocks
    sub = lax.broadcasted_iota(jnp.int32, (BS, 2 * BS), 0)
    lane = lax.broadcasted_iota(jnp.int32, (BS, 2 * BS), 1)
    left = lane < BS
    size_col = jnp.where(left, sizes[first_col], sizes[first_col + 1])
    valid_col = (jnp.where(left, lane, lane - BS) < size_col).astype(F32)
    for i in range(row_blocks):
        stored = jnp.where(left, pattern[0, i], pattern[1, i]).astype(F32)
        valid = (sub < sizes[first_row + i]).astype(F32) * valid_col * stored
        out[i * BS : (i + 1) * BS, :] = density[i * BS : (i + 1) * BS, :] * valid


def split(x):
    hi = x.astype(BF16)
    return hi, (x - hi.astype(F32)).astype(BF16)


def product_kernel(plan, has_acc, last, *refs):
    n_in = 1 + sum(1 if kind == "both" else 2 for kind, _ in plan)
    right = refs[0]
    acc = refs[n_in][...] if has_acc else None
    outs = refs[n_in + has_acc :]
    z = lax.axis_index("z")
    c = lax.axis_index("c")

    def unit(u):
        y = u // 3
        rows = pl.ds(pl.multiple_of((u - 3 * y) * 128, 128), 128)
        return jnp.concatenate([right[y, 0, rows, :], right[y, 1, rows, :]], axis=1)

    dot = functools.partial(jnp.dot, preferred_element_type=F32)
    at = 1
    for kind, offsets in plan:
        for k, off in enumerate(offsets):
            zz = lax.rem(z + (off + NZ), NZ)
            if kind == "both":
                a = jnp.concatenate([refs[at][0], refs[at][1]], axis=1)
                first, second = 2 * zz, 2 * zz + 1
            else:
                a = jnp.concatenate([refs[at][k], refs[at + 1][k]], axis=1)
                first, second = 2 * zz + c, 2 * zz + 1 - c
            b = jnp.concatenate([unit(first), unit(second)], axis=0)
            ah, al = split(a)
            bh, bl = split(b)
            term = dot(ah, bh) + (dot(ah, bl) + dot(al, bh))
            acc = term if acc is None else acc + term
        at += 1 if kind == "both" else 2
    if not last:
        outs[0][...] = acc
        return
    same = lax.axis_index("xl") == lax.axis_index("xh")
    near, far = acc[:, :128], acc[:, 128:]
    outs[0][...] = jnp.where(same, near, far)
    outs[1][...] = jnp.where(same, far, near)


def product(right, groups, acc=None, last=True):
    plan = tuple((kind, offsets) for kind, offsets, _ in groups)
    n = sum(len(offsets) for _, offsets in plan)
    rows, cols = groups[0][2][0].shape[1:]
    args = [right] + [x for _, _, arrays in groups for x in arrays]
    if acc is not None:
        args.append(acc)
    if last:
        shapes = (jax.ShapeDtypeStruct((rows, cols), F32),) * 2
    else:
        shapes = jax.ShapeDtypeStruct((rows, 2 * cols), F32)
    return pl.pallas_call(
        functools.partial(product_kernel, plan, acc is not None, last),
        out_shape=shapes,
        in_specs=[VM] * len(args),
        out_specs=(VM, VM) if last else VM,
        compiler_params=PARAMS,
        cost_estimate=pl.CostEstimate(
            flops=n * 3 * 2 * rows * 2 * cols * 2 * cols, bytes_accessed=0, transcendentals=0
        ),
    )(*args)


def first_kernel(offsets, left, *refs):
    n = len(offsets)
    near, far = refs[:n], refs[n : 2 * n]
    mine, other, right = refs[2 * n :]
    y = lax.axis_index("y")
    dot = functools.partial(jnp.dot, preferred_element_type=F32)
    acc = None
    for k, off in enumerate(offsets):
        yy = lax.rem(y + (off + NY), NY)
        u = 3 * yy
        a = jnp.concatenate([left[u], left[u + 1], left[u + 2]], axis=1)
        right[yy, 0] = near[k][...]
        right[yy, 1] = far[k][...]
        b = jnp.concatenate([near[k][...], far[k][...]], axis=1)
        ah, al = split(a)
        bh, bl = split(b)
        term = dot(ah, bh) + (dot(ah, bl) + dot(al, bh))
        acc = term if acc is None else acc + term
    same = lax.axis_index("xl") == lax.axis_index("xh")
    first, second = acc[:, :128], acc[:, 128:]
    mine[...] = jnp.where(same, first, second)
    other[...] = jnp.where(same, second, first)


def first_product(left, offsets, near, far):
    rows, cols = near[0].shape
    block = jax.ShapeDtypeStruct((rows, cols), F32)
    args = [left] + near + far
    mine, other, right = pl.pallas_call(
        functools.partial(first_kernel, tuple(offsets)),
        out_shape=(block, block, jax.ShapeDtypeStruct((NY, 2, rows, cols), F32)),
        in_specs=[VM] * len(args),
        out_specs=(VM, VM, VM),
        compiler_params=PARAMS,
        cost_estimate=pl.CostEstimate(
            flops=NY * 3 * 2 * rows * rows * 2 * cols, bytes_accessed=0, transcendentals=0
        ),
    )(*args)
    return (mine, other), right


def filter_kernel(final, kept, mine, pair, *refs):
    other = 1 - lax.axis_index("xl")
    lane = lax.broadcasted_iota(jnp.int32, (BS, 2 * BS), 1)
    for i in range(kept.shape[1]):
        strip = slice(i * BS, (i + 1) * BS)
        filt = jnp.where(lane < BS, kept[0, i], kept[1, i]).astype(F32)
        total = filt * (mine[strip, :] + pair[other, strip, :])
        if final:
            refs[1][strip, :] = 3.0 * refs[0][strip, :] - 2.0 * total
        else:
            refs[0][strip, :] = total


def filtered(kept, halves, square=None):
    mine, other = halves
    pair = lax.all_gather(other, "xl", axis=0)
    args = [kept, mine, pair] + ([] if square is None else [square])
    return pl.pallas_call(
        functools.partial(filter_kernel, square is not None),
        out_shape=jax.ShapeDtypeStruct(mine.shape, F32),
        in_specs=[SM] + [VM] * (len(args) - 1),
        out_specs=VM,
        compiler_params=PARAMS,
    )(*args)


def shift(x, axis, step):
    n = SIZES[AXES.index(axis)]
    return lax.ppermute(x, axis, [(i, (i + step) % n) for i in range(n)])


def together(*xs):
    return lax.optimization_barrier(xs)


def chain(x, axis, step, count):
    out = []
    for _ in range(count):
        x = shift(x, axis, step)
        out.append(x)
    return out


def body(density, atom_sizes, pattern, kept):
    masked = pl.pallas_call(
        mask_kernel,
        out_shape=jax.ShapeDtypeStruct(density.shape, F32),
        in_specs=[SM, SM, VM],
        out_specs=VM,
        compiler_params=PARAMS,
    )(atom_sizes, pattern.T, density)

    left = lax.all_gather(masked, ("z", "c"), axis=0)

    near = lax.ppermute(masked, ("xh", "xl"), [(0, 0), (1, 2), (2, 1), (3, 3)])
    far = lax.ppermute(masked, ("xh", "xl"), [(1, 0), (2, 3), (0, 2), (3, 1)])
    near_up, near_down = chain(near, "y", 1, 4), chain(near, "y", -1, 3)
    far_up, far_down = chain(far, "y", 1, 3), chain(far, "y", -1, 4)
    offsets = [0, -1, 1, -2, 2, -3, 3, 4]
    near = [near] + [x for pair in zip(near_up, near_down) for x in pair] + [near_up[3]]
    far = [far] + [x for pair in zip(far_up, far_down) for x in pair] + [far_down[3]]
    halves, right = first_product(left, offsets, near, far)
    square = filtered(kept.T, halves)

    up, down = chain(square, "z", 1, 6), chain(square, "z", -1, 5)
    most = jnp.stack([square] + [x for pair in zip(up[:4], down[:4]) for x in pair])
    most_sib = shift(most, "c", 1)
    some = jnp.stack([up[4], down[4], up[5]])
    some_sib = shift(some, "c", 1)
    acc = product(right, [("pair", (0, -1, 1, -2, 2, -3, 3, -4, 4), (most, most_sib))], last=False)
    halves = product(right, [("pair", (-5, 5, -6), (some, some_sib))], acc)
    purified = filtered(kept.T, halves, square)
    return (square, purified)


def solution(mesh):
    fine = Mesh(mesh.devices.reshape(SIZES), AXES)
    placed = (P(ROW, COL), P(), P(ROW, COL), P(ROW, COL))
    return jax.shard_map(
        body,
        mesh=fine,
        in_specs=placed,
        out_specs=(P(ROW, COL), P(ROW, COL)),
        check_vma=False,
    )
```

```python
import functools

import jax
import jax.numpy as jnp
from jax import lax
from jax.experimental import pallas as pl
from jax.experimental.pallas import tpu as pltpu
from jax.sharding import Mesh, PartitionSpec as P

BS = 64
AXES = ("xh", "y", "xl", "z", "c")
SIZES = (2, 8, 2, 12, 2)
NY = 8
NZ = 12
ROW = ("xh", "y")
COL = ("xl", "z", "c")
F32 = jnp.float32
BF16 = jnp.bfloat16
VM = pl.BlockSpec(memory_space=pltpu.VMEM)
SM = pl.BlockSpec(memory_space=pltpu.SMEM)
HB = pl.BlockSpec(memory_space=pltpu.HBM)
PARAMS = pltpu.CompilerParams(vmem_limit_bytes=32 * 1024 * 1024)
WIDE = pltpu.CompilerParams(vmem_limit_bytes=50 * 1024 * 1024)
WHOLE = pltpu.CompilerParams(vmem_limit_bytes=64 * 1024 * 1024 - 128 * 1024)


def mask_kernel(sizes_hbm, pattern_hbm, density_hbm, out, sizes, pattern, density, sems):
    copies = [
        pltpu.make_async_copy(sizes_hbm, sizes, sems.at[0]),
        pltpu.make_async_copy(pattern_hbm, pattern, sems.at[1]),
        pltpu.make_async_copy(density_hbm, density, sems.at[2]),
    ]
    for copy in copies:
        copy.start()
    col_blocks, row_blocks = pattern.shape
    first_row = (lax.axis_index("xh") * NY + lax.axis_index("y")) * row_blocks
    first_col = ((lax.axis_index("xl") * NZ + lax.axis_index("z")) * 2 + lax.axis_index("c")) * col_blocks
    sub = lax.broadcasted_iota(jnp.int32, (BS, 2 * BS), 0)
    lane = lax.broadcasted_iota(jnp.int32, (BS, 2 * BS), 1)
    left = lane < BS
    for copy in copies:
        copy.wait()
    size_col = jnp.where(left, sizes[first_col], sizes[first_col + 1])
    valid_col = (jnp.where(left, lane, lane - BS) < size_col).astype(F32)
    for i in range(row_blocks):
        stored = jnp.where(left, pattern[0, i], pattern[1, i]).astype(F32)
        valid = (sub < sizes[first_row + i]).astype(F32) * valid_col * stored
        out[i * BS : (i + 1) * BS, :] = density[i * BS : (i + 1) * BS, :] * valid


def split(x):
    hi = x.astype(BF16)
    return hi, (x - hi.astype(F32)).astype(BF16)


dot = functools.partial(jnp.dot, preferred_element_type=F32)


def split_dot(a, b):
    ah, al = split(a)
    bh, bl = split(b)
    return dot(ah, bh) + (dot(ah, bl) + dot(al, bh))


def put_halves(total, mine, other):
    same = lax.axis_index("xl") == lax.axis_index("xh")
    near, far = total[:, :128], total[:, 128:]
    mine[...] = jnp.where(same, near, far)
    other[...] = jnp.where(same, far, near)


def pack_kernel(offsets, *refs):
    n = len(offsets)
    near, far = refs[:n], refs[n : 2 * n]
    right, give = refs[2 * n :]
    y = lax.axis_index("y")
    for k, off in enumerate(offsets):
        first = 3 * lax.rem(y + (off + NY), NY)
        for t in range(3):
            rows = slice(t * 128, (t + 1) * 128)
            right[first + t, :, :128] = near[k][rows, :]
            right[first + t, :, 128:] = far[k][rows, :]
    c = lax.axis_index("c")
    for z in range(NZ):
        give[z] = right[2 * z + 1 - c]


def pack(offsets, near, far):
    rows, cols = near[0].shape
    args = near + far
    return pl.pallas_call(
        functools.partial(pack_kernel, tuple(offsets)),
        out_shape=(
            jax.ShapeDtypeStruct((2 * NZ, 128, 2 * cols), F32),
            jax.ShapeDtypeStruct((NZ, 128, 2 * cols), F32),
        ),
        in_specs=[VM] * len(args),
        out_specs=(VM, VM),
        compiler_params=PARAMS,
    )(*args)


def first_kernel(left, right, mine, other, held, sems):
    copies = [pltpu.make_async_copy(left.at[pl.ds(2 * z, 2)], held.at[z], sems.at[z]) for z in range(NZ)]
    for copy in copies:
        copy.start()
    acc = None
    for z in range(NZ):
        copies[z].wait()
        a = jnp.concatenate([held[z, 0], held[z, 1]], axis=1)
        b = jnp.concatenate([right[2 * z], right[2 * z + 1]], axis=0)
        term = split_dot(a, b)
        acc = term if acc is None else acc + term
    put_halves(acc, mine, other)


def first_product(left, right):
    _, rows, cols = left.shape
    block = jax.ShapeDtypeStruct((rows, cols), F32)
    return pl.pallas_call(
        first_kernel,
        out_shape=(block, block),
        in_specs=[HB, VM],
        out_specs=(VM, VM),
        scratch_shapes=[pltpu.VMEM((NZ, 2, rows, cols), F32), pltpu.SemaphoreType.DMA((NZ,))],
        compiler_params=WIDE,
        cost_estimate=pl.CostEstimate(
            flops=NZ * 3 * 2 * rows * 2 * cols * 2 * cols, bytes_accessed=0, transcendentals=0
        ),
    )(left, right)


def second_kernel(offsets, has_acc, last, right, took, *refs):
    n = len(offsets)
    acc = refs[n][...] if has_acc else None
    outs = refs[n + has_acc :]
    z = lax.axis_index("z")
    c = lax.axis_index("c")

    def rows(off):
        zz = lax.rem(z + (off + NZ), NZ)
        return jnp.concatenate([right[2 * zz + c], took[zz]], axis=1)

    for k in range(0, n, 2):
        a = jnp.concatenate([refs[k][...], refs[k + 1][...]], axis=1)
        b = jnp.concatenate([rows(offsets[k]), rows(offsets[k + 1])], axis=0)
        term = split_dot(a, b)
        acc = term if acc is None else acc + term
    if last:
        outs[0][...] = acc[:, :256]
        outs[1][...] = acc[:, 256:]
    else:
        outs[0][...] = acc


def second_product(right, took, blocks, acc=None, last=False):
    offsets = tuple(off for off, _ in blocks)
    rows, cols = blocks[0][1].shape
    args = [right, took] + [x for _, x in blocks] + ([] if acc is None else [acc])
    if last:
        shapes = (jax.ShapeDtypeStruct((rows, 2 * cols), F32),) * 2
    else:
        shapes = jax.ShapeDtypeStruct((rows, 4 * cols), F32)
    return pl.pallas_call(
        functools.partial(second_kernel, offsets, acc is not None, last),
        out_shape=shapes,
        in_specs=[VM] * len(args),
        out_specs=(VM, VM) if last else VM,
        compiler_params=PARAMS,
        cost_estimate=pl.CostEstimate(
            flops=len(offsets) * 3 * 2 * rows * cols * 4 * cols, bytes_accessed=0, transcendentals=0
        ),
    )(*args)


def join_kernel(own, both, mine, other):
    put_halves(own[...] + both[1 - lax.axis_index("c")], mine, other)


def join(own, give):
    both = lax.all_gather(give, "c", axis=0)
    rows, cols = own.shape
    block = jax.ShapeDtypeStruct((rows, cols // 2), F32)
    return pl.pallas_call(
        join_kernel,
        out_shape=(block, block),
        in_specs=[VM, VM],
        out_specs=(VM, VM),
        compiler_params=PARAMS,
    )(own, both)


def filter_kernel(final, kept, mine, pair, *refs):
    other = 1 - lax.axis_index("xl")
    lane = lax.broadcasted_iota(jnp.int32, (BS, 2 * BS), 1)
    for i in range(kept.shape[1]):
        strip = slice(i * BS, (i + 1) * BS)
        filt = jnp.where(lane < BS, kept[0, i], kept[1, i]).astype(F32)
        total = filt * (mine[strip, :] + pair[other, strip, :])
        if final:
            refs[1][strip, :] = 3.0 * refs[0][strip, :] - 2.0 * total
        else:
            refs[0][strip, :] = total


def filtered(kept, halves, square=None):
    mine, other = halves
    pair = lax.all_gather(other, "xl", axis=0)
    args = [kept, mine, pair] + ([] if square is None else [square])
    return pl.pallas_call(
        functools.partial(filter_kernel, square is not None),
        out_shape=jax.ShapeDtypeStruct(mine.shape, F32),
        in_specs=[SM] + [VM] * (len(args) - 1),
        out_specs=VM,
        compiler_params=PARAMS,
    )(*args)


def shift(x, axis, step):
    n = SIZES[AXES.index(axis)]
    return lax.ppermute(x, axis, [(i, (i + step) % n) for i in range(n)])


def together(*xs):
    return lax.optimization_barrier(xs)


def chain(x, axis, step, count):
    out = []
    for _ in range(count):
        x = shift(x, axis, step)
        out.append(x)
    return out


def body(density, atom_sizes, pattern, kept):
    pattern = pattern.T
    masked = pl.pallas_call(
        mask_kernel,
        out_shape=jax.ShapeDtypeStruct(density.shape, F32),
        in_specs=[HB] * 3,
        out_specs=VM,
        scratch_shapes=[
            pltpu.SMEM(atom_sizes.shape, jnp.int32),
            pltpu.SMEM(pattern.shape, jnp.int32),
            pltpu.VMEM(density.shape, F32),
            pltpu.SemaphoreType.DMA((3,)),
        ],
        compiler_params=WHOLE,
    )(atom_sizes, pattern, density)

    left = lax.all_gather(masked, ("z", "c"), axis=0)

    near = lax.ppermute(masked, ("xh", "xl"), [(0, 0), (1, 2), (2, 1), (3, 3)])
    far = lax.ppermute(masked, ("xh", "xl"), [(1, 0), (2, 3), (0, 2), (3, 1)])
    near_up, near_down = chain(near, "y", 1, 4), chain(near, "y", -1, 3)
    far_up, far_down = chain(far, "y", 1, 3), chain(far, "y", -1, 4)
    offsets = [0, -1, 1, -2, 2, -3, 3, 4]
    near = [near] + [x for pair in zip(near_up, near_down) for x in pair] + [near_up[3]]
    far = [far] + [x for pair in zip(far_up, far_down) for x in pair] + [far_down[3]]
    right, give = pack(offsets, near, far)
    took = shift(give, "c", 1)
    mine, other, took = together(*first_product(left, right), took)
    square = filtered(kept.T, (mine, other))

    up, down = chain(square, "z", 1, 6), chain(square, "z", -1, 5)
    blocks = [(0, square)]
    for s in range(5):
        blocks += [(-s - 1, up[s]), (s + 1, down[s])]
    blocks.append((-6, up[5]))
    acc = second_product(right, took, blocks[:4])
    acc = second_product(right, took, blocks[4:8], acc)
    halves = join(*second_product(right, took, blocks[8:], acc, last=True))
    purified = filtered(kept.T, halves, square)
    return (square, purified)


def solution(mesh):
    fine = Mesh(mesh.devices.reshape(SIZES), AXES)
    placed = (P(ROW, COL), P(), P(ROW, COL), P(ROW, COL))
    return jax.shard_map(
        body,
        mesh=fine,
        in_specs=placed,
        out_specs=(P(ROW, COL), P(ROW, COL)),
        check_vma=False,
    )
```

```python
import functools

import jax
import jax.numpy as jnp
from jax import lax
from jax.experimental import pallas as pl
from jax.experimental.pallas import tpu as pltpu
from jax.sharding import Mesh, PartitionSpec as P

BS = 64
AXES = ("xh", "y", "xl", "z", "c")
SIZES = (2, 8, 2, 12, 2)
NY = 8
NZ = 12
ROW = ("xh", "y")
COL = ("xl", "z", "c")
F32 = jnp.float32
BF16 = jnp.bfloat16
VM = pl.BlockSpec(memory_space=pltpu.VMEM)
SM = pl.BlockSpec(memory_space=pltpu.SMEM)
HB = pl.BlockSpec(memory_space=pltpu.HBM)
PARAMS = pltpu.CompilerParams(vmem_limit_bytes=32 * 1024 * 1024)
WIDE = pltpu.CompilerParams(vmem_limit_bytes=50 * 1024 * 1024)
WHOLE = pltpu.CompilerParams(vmem_limit_bytes=64 * 1024 * 1024 - 128 * 1024)


def mask_kernel(sizes_hbm, pattern_hbm, density_hbm, out, sizes, pattern, density, sems):
    copies = [
        pltpu.make_async_copy(sizes_hbm, sizes, sems.at[0]),
        pltpu.make_async_copy(pattern_hbm, pattern, sems.at[1]),
        pltpu.make_async_copy(density_hbm, density, sems.at[2]),
    ]
    for copy in copies:
        copy.start()
    col_blocks, row_blocks = pattern.shape
    first_row = (lax.axis_index("xh") * NY + lax.axis_index("y")) * row_blocks
    first_col = ((lax.axis_index("xl") * NZ + lax.axis_index("z")) * 2 + lax.axis_index("c")) * col_blocks
    sub = lax.broadcasted_iota(jnp.int32, (BS, 2 * BS), 0)
    lane = lax.broadcasted_iota(jnp.int32, (BS, 2 * BS), 1)
    left = lane < BS
    for copy in copies:
        copy.wait()
    size_col = jnp.where(left, sizes[first_col], sizes[first_col + 1])
    valid_col = (jnp.where(left, lane, lane - BS) < size_col).astype(F32)
    for i in range(row_blocks):
        stored = jnp.where(left, pattern[0, i], pattern[1, i]).astype(F32)
        valid = (sub < sizes[first_row + i]).astype(F32) * valid_col * stored
        out[i * BS : (i + 1) * BS, :] = density[i * BS : (i + 1) * BS, :] * valid


def split(x):
    hi = x.astype(BF16)
    return hi, (x - hi.astype(F32)).astype(BF16)


dot = functools.partial(jnp.dot, preferred_element_type=F32)


def split_dot(a, bh, bl):
    ah, al = split(a)
    return dot(ah, bh) + (dot(ah, bl) + dot(al, bh))


def put_halves(total, mine, other):
    same = lax.axis_index("xl") == lax.axis_index("xh")
    near, far = total[:, :128], total[:, 128:]
    mine[...] = jnp.where(same, near, far)
    other[...] = jnp.where(same, far, near)


def pack_kernel(offsets, *refs):
    n = len(offsets)
    near, far = refs[:n], refs[n : 2 * n]
    hi, lo, give = refs[2 * n :]
    y = lax.axis_index("y")
    c = lax.axis_index("c")
    for k, off in enumerate(offsets):
        first = 3 * lax.rem(y + (off + NY), NY)
        for t in range(3):
            rows = slice(t * 128, (t + 1) * 128)
            unit = jnp.concatenate([near[k][rows, :], far[k][rows, :]], axis=1)
            hi[first + t], lo[first + t] = split(unit)

            @pl.when(lax.rem(first + t, 2) != c)
            def _():
                give[(first + t) // 2] = unit


def pack(offsets, near, far):
    rows, cols = near[0].shape
    args = near + far
    half = jax.ShapeDtypeStruct((2 * NZ, 128, 2 * cols), BF16)
    return pl.pallas_call(
        functools.partial(pack_kernel, tuple(offsets)),
        out_shape=(half, half, jax.ShapeDtypeStruct((NZ, 128, 2 * cols), F32)),
        in_specs=[VM] * len(args),
        out_specs=(VM,) * 3,
        compiler_params=PARAMS,
    )(*args)


def rows_kernel(hi, lo, took, rows_hi, rows_lo):
    c = lax.axis_index("c")
    for z in range(NZ):
        rows_hi[z, :, :256] = hi[2 * z + c]
        rows_lo[z, :, :256] = lo[2 * z + c]
        rows_hi[z, :, 256:], rows_lo[z, :, 256:] = split(took[z])


def phase_rows(hi, lo, took):
    units, depth, cols = took.shape
    half = jax.ShapeDtypeStruct((units, depth, 2 * cols), BF16)
    return pl.pallas_call(
        rows_kernel,
        out_shape=(half, half),
        in_specs=[VM] * 3,
        out_specs=(VM, VM),
        compiler_params=PARAMS,
    )(hi, lo, took)


def first_kernel(left, hi, lo, mine, other, held, sems):
    parts, per = held.shape[:2]
    copies = [
        pltpu.make_async_copy(left.at[pl.ds(per * p, per)], held.at[p], sems.at[p]) for p in range(parts)
    ]
    for p in range(3):
        copies[p].start()
    acc = None
    for p in range(parts):
        copies[p].wait()
        if p + 3 < parts:
            copies[p + 3].start()
        for k in range(0, per, 2):
            u = per * p + k
            a = jnp.concatenate([held[p, k], held[p, k + 1]], axis=1)
            bh = jnp.concatenate([hi[u], hi[u + 1]], axis=0)
            bl = jnp.concatenate([lo[u], lo[u + 1]], axis=0)
            term = split_dot(a, bh, bl)
            acc = term if acc is None else acc + term
    put_halves(acc, mine, other)


def first_product(left, hi, lo):
    units, rows, cols = left.shape
    parts = 6
    block = jax.ShapeDtypeStruct((rows, cols), F32)
    return pl.pallas_call(
        first_kernel,
        out_shape=(block, block),
        in_specs=[HB, VM, VM],
        out_specs=(VM, VM),
        scratch_shapes=[
            pltpu.VMEM((parts, units // parts, rows, cols), F32),
            pltpu.SemaphoreType.DMA((parts,)),
        ],
        compiler_params=WIDE,
        cost_estimate=pl.CostEstimate(
            flops=NZ * 3 * 2 * rows * 2 * cols * 2 * cols, bytes_accessed=0, transcendentals=0
        ),
    )(left, hi, lo)


def second_kernel(offsets, has_acc, last, hi, lo, *refs):
    n = len(offsets)
    acc = refs[n][...] if has_acc else None
    outs = refs[n + has_acc :]
    z = lax.axis_index("z")
    sign = 1 - 2 * lax.axis_index("c")
    at = [lax.rem(z + sign * off + NZ, NZ) for off in offsets]
    for k in range(0, n, 2):
        a = jnp.concatenate([refs[k][...], refs[k + 1][...]], axis=1)
        bh = jnp.concatenate([hi[at[k]], hi[at[k + 1]]], axis=0)
        bl = jnp.concatenate([lo[at[k]], lo[at[k + 1]]], axis=0)
        term = split_dot(a, bh, bl)
        acc = term if acc is None else acc + term
    if last:
        outs[0][...] = acc[:, :256]
        outs[1][...] = acc[:, 256:]
    else:
        outs[0][...] = acc


def second_product(operand, blocks, acc=None, last=False):
    offsets = tuple(off for off, _ in blocks)
    rows, cols = blocks[0][1].shape
    args = list(operand) + [x for _, x in blocks] + ([] if acc is None else [acc])
    if last:
        shapes = (jax.ShapeDtypeStruct((rows, 2 * cols), F32),) * 2
    else:
        shapes = jax.ShapeDtypeStruct((rows, 4 * cols), F32)
    return pl.pallas_call(
        functools.partial(second_kernel, offsets, acc is not None, last),
        out_shape=shapes,
        in_specs=[VM] * len(args),
        out_specs=(VM, VM) if last else VM,
        compiler_params=PARAMS,
        cost_estimate=pl.CostEstimate(
            flops=len(offsets) * 3 * 2 * rows * cols * 4 * cols, bytes_accessed=0, transcendentals=0
        ),
    )(*args)


def join_kernel(own, both, mine, other):
    put_halves(own[...] + both[1 - lax.axis_index("c")], mine, other)


def join(own, give):
    both = lax.all_gather(give, "c", axis=0)
    rows, cols = own.shape
    block = jax.ShapeDtypeStruct((rows, cols // 2), F32)
    return pl.pallas_call(
        join_kernel,
        out_shape=(block, block),
        in_specs=[VM, VM],
        out_specs=(VM, VM),
        compiler_params=PARAMS,
    )(own, both)


def filter_kernel(final, kept, mine, pair, *refs):
    other = 1 - lax.axis_index("xl")
    lane = lax.broadcasted_iota(jnp.int32, (BS, 2 * BS), 1)
    for i in range(kept.shape[1]):
        strip = slice(i * BS, (i + 1) * BS)
        filt = jnp.where(lane < BS, kept[0, i], kept[1, i]).astype(F32)
        total = filt * (mine[strip, :] + pair[other, strip, :])
        if final:
            refs[1][strip, :] = 3.0 * refs[0][strip, :] - 2.0 * total
        else:
            refs[0][strip, :] = total


def filtered(kept, halves, square=None):
    mine, other = halves
    pair = lax.all_gather(other, "xl", axis=0)
    args = [kept, mine, pair] + ([] if square is None else [square])
    return pl.pallas_call(
        functools.partial(filter_kernel, square is not None),
        out_shape=jax.ShapeDtypeStruct(mine.shape, F32),
        in_specs=[SM] + [VM] * (len(args) - 1),
        out_specs=VM,
        compiler_params=PARAMS,
    )(*args)


def shift(x, axis, step):
    n = SIZES[AXES.index(axis)]
    return lax.ppermute(x, axis, [(i, (i + step) % n) for i in range(n)])


def together(*xs):
    return lax.optimization_barrier(xs)


def chain(x, axis, step, count):
    out = []
    for _ in range(count):
        x = shift(x, axis, step)
        out.append(x)
    return out


def zchain(x, steps, count):
    pairs = [(2 * z + c, 2 * ((z + steps[c]) % NZ) + c) for z in range(NZ) for c in range(2)]
    out = []
    for _ in range(count):
        x = lax.ppermute(x, ("z", "c"), pairs)
        out.append(x)
    return out


def body(density, atom_sizes, pattern, kept):
    pattern = pattern.T
    masked = pl.pallas_call(
        mask_kernel,
        out_shape=jax.ShapeDtypeStruct(density.shape, F32),
        in_specs=[HB] * 3,
        out_specs=VM,
        scratch_shapes=[
            pltpu.SMEM(atom_sizes.shape, jnp.int32),
            pltpu.SMEM(pattern.shape, jnp.int32),
            pltpu.VMEM(density.shape, F32),
            pltpu.SemaphoreType.DMA((3,)),
        ],
        compiler_params=WHOLE,
    )(atom_sizes, pattern, density)

    left = lax.all_gather(masked, ("z", "c"), axis=0)

    near = lax.ppermute(masked, ("xh", "xl"), [(0, 0), (1, 2), (2, 1), (3, 3)])
    far = lax.ppermute(masked, ("xh", "xl"), [(1, 0), (2, 3), (0, 2), (3, 1)])
    near_up, near_down = chain(near, "y", 1, 4), chain(near, "y", -1, 3)
    far_up, far_down = chain(far, "y", 1, 3), chain(far, "y", -1, 4)
    offsets = [0, -1, 1, -2, 2, -3, 3, 4]
    near = [near] + [x for pair in zip(near_up, near_down) for x in pair] + [near_up[3]]
    far = [far] + [x for pair in zip(far_up, far_down) for x in pair] + [far_down[3]]
    hi, lo, give = pack(offsets, near, far)
    took = shift(give, "c", 1)
    mine, other, took = together(*first_product(left, hi, lo), took)
    square = filtered(kept.T, (mine, other))

    operand = phase_rows(hi, lo, took)
    ahead, back = zchain(square, (1, -1), 6), zchain(square, (-1, 1), 5)
    blocks = [(0, square)]
    for s in range(5):
        blocks += [(-s - 1, ahead[s]), (s + 1, back[s])]
    blocks.append((-6, ahead[5]))
    acc = second_product(operand, blocks[:4])
    acc = second_product(operand, blocks[4:8], acc)
    halves = join(*second_product(operand, blocks[8:], acc, last=True))
    purified = filtered(kept.T, halves, square)
    return (square, purified)


def solution(mesh):
    fine = Mesh(mesh.devices.reshape(SIZES), AXES)
    placed = (P(ROW, COL), P(), P(ROW, COL), P(ROW, COL))
    return jax.shard_map(
        body,
        mesh=fine,
        in_specs=placed,
        out_specs=(P(ROW, COL), P(ROW, COL)),
        check_vma=False,
    )
```

```python
import functools

import jax
import jax.numpy as jnp
from jax import lax
from jax.experimental import pallas as pl
from jax.experimental.pallas import tpu as pltpu
from jax.sharding import Mesh, PartitionSpec as P

BS = 64
AXES = ("xh", "y", "xl", "z", "c")
SIZES = (2, 8, 2, 12, 2)
NY = 8
NZ = 12
ROW = ("xh", "y")
COL = ("xl", "z", "c")
F32 = jnp.float32
BF16 = jnp.bfloat16
VM = pl.BlockSpec(memory_space=pltpu.VMEM)
SM = pl.BlockSpec(memory_space=pltpu.SMEM)
HB = pl.BlockSpec(memory_space=pltpu.HBM)
PARAMS = pltpu.CompilerParams(vmem_limit_bytes=32 * 1024 * 1024)
WIDE = pltpu.CompilerParams(vmem_limit_bytes=50 * 1024 * 1024)
WHOLE = pltpu.CompilerParams(vmem_limit_bytes=64 * 1024 * 1024 - 128 * 1024)


def mask_kernel(sizes_hbm, pattern_hbm, density_hbm, out, sizes, pattern, density, sems):
    copies = [
        pltpu.make_async_copy(sizes_hbm, sizes, sems.at[0]),
        pltpu.make_async_copy(pattern_hbm, pattern, sems.at[1]),
        pltpu.make_async_copy(density_hbm, density, sems.at[2]),
    ]
    for copy in copies:
        copy.start()
    col_blocks, row_blocks = pattern.shape
    first_row = (lax.axis_index("xh") * NY + lax.axis_index("y")) * row_blocks
    first_col = ((lax.axis_index("xl") * NZ + lax.axis_index("z")) * 2 + lax.axis_index("c")) * col_blocks
    sub = lax.broadcasted_iota(jnp.int32, (BS, 2 * BS), 0)
    lane = lax.broadcasted_iota(jnp.int32, (BS, 2 * BS), 1)
    left = lane < BS
    for copy in copies:
        copy.wait()
    size_col = jnp.where(left, sizes[first_col], sizes[first_col + 1])
    valid_col = (jnp.where(left, lane, lane - BS) < size_col).astype(F32)
    for i in range(row_blocks):
        stored = jnp.where(left, pattern[0, i], pattern[1, i]).astype(F32)
        valid = (sub < sizes[first_row + i]).astype(F32) * valid_col * stored
        out[i * BS : (i + 1) * BS, :] = density[i * BS : (i + 1) * BS, :] * valid


def split(x):
    hi = x.astype(BF16)
    return hi, (x - hi.astype(F32)).astype(BF16)


dot = functools.partial(jnp.dot, preferred_element_type=F32)


def split_dot(a, bh, bl):
    ah, al = split(a)
    return dot(ah, bh) + (dot(ah, bl) + dot(al, bh))


def put_halves(total, mine, other):
    same = lax.axis_index("xl") == lax.axis_index("xh")
    near, far = total[:, :128], total[:, 128:]
    mine[...] = jnp.where(same, near, far)
    other[...] = jnp.where(same, far, near)


def pack_kernel(offsets, *refs):
    n = len(offsets)
    near, far = refs[:n], refs[n : 2 * n]
    hi, lo, give = refs[2 * n :]
    y = lax.axis_index("y")
    c = lax.axis_index("c")
    for k, off in enumerate(offsets):
        first = 3 * lax.rem(y + (off + NY), NY)
        for t in range(3):
            rows = slice(t * 128, (t + 1) * 128)
            unit = jnp.concatenate([near[k][rows, :], far[k][rows, :]], axis=1)
            hi[first + t], lo[first + t] = split(unit)

            @pl.when(lax.rem(first + t, 2) != c)
            def _():
                give[(first + t) // 2] = unit


def pack(offsets, near, far):
    rows, cols = near[0].shape
    args = near + far
    half = jax.ShapeDtypeStruct((2 * NZ, 128, 2 * cols), BF16)
    return pl.pallas_call(
        functools.partial(pack_kernel, tuple(offsets)),
        out_shape=(half, half, jax.ShapeDtypeStruct((NZ, 128, 2 * cols), F32)),
        in_specs=[VM] * len(args),
        out_specs=(VM,) * 3,
        compiler_params=PARAMS,
    )(*args)


def rows_kernel(hi, lo, took, rows_hi, rows_lo):
    c = lax.axis_index("c")
    for z in range(NZ):
        rows_hi[z, :, :256] = hi[2 * z + c]
        rows_lo[z, :, :256] = lo[2 * z + c]
        rows_hi[z, :, 256:], rows_lo[z, :, 256:] = split(took[z])


def phase_rows(hi, lo, took):
    units, depth, cols = took.shape
    half = jax.ShapeDtypeStruct((units, depth, 2 * cols), BF16)
    return pl.pallas_call(
        rows_kernel,
        out_shape=(half, half),
        in_specs=[VM] * 3,
        out_specs=(VM, VM),
        compiler_params=PARAMS,
    )(hi, lo, took)


def first_kernel(left, hi, lo, mine, other, held, sems):
    parts, per = held.shape[:2]
    copies = [
        pltpu.make_async_copy(left.at[pl.ds(per * p, per)], held.at[p], sems.at[p]) for p in range(parts)
    ]
    for copy in copies:
        copy.start()
    for copy in copies:
        copy.wait()
    acc = None
    for z in range(NZ):
        u = 2 * z
        p, k = divmod(u, per)
        a = jnp.concatenate([held[p, k], held[p, k + 1]], axis=1)
        bh = jnp.concatenate([hi[u], hi[u + 1]], axis=0)
        bl = jnp.concatenate([lo[u], lo[u + 1]], axis=0)
        term = split_dot(a, bh, bl)
        acc = term if acc is None else acc + term
    put_halves(acc, mine, other)


def first_product(left, hi, lo):
    units, rows, cols = left.shape
    parts = 6
    block = jax.ShapeDtypeStruct((rows, cols), F32)
    return pl.pallas_call(
        first_kernel,
        out_shape=(block, block),
        in_specs=[HB, VM, VM],
        out_specs=(VM, VM),
        scratch_shapes=[
            pltpu.VMEM((parts, units // parts, rows, cols), F32),
            pltpu.SemaphoreType.DMA((parts,)),
        ],
        compiler_params=WIDE,
        cost_estimate=pl.CostEstimate(
            flops=NZ * 3 * 2 * rows * 2 * cols * 2 * cols, bytes_accessed=0, transcendentals=0
        ),
    )(left, hi, lo)


def second_kernel(offsets, has_acc, last, hi, lo, *refs):
    n = len(offsets)
    acc = refs[n][...] if has_acc else None
    outs = refs[n + has_acc :]
    z = lax.axis_index("z")
    at = [lax.rem(z + (off + NZ), NZ) for off in offsets]
    for k in range(0, n, 2):
        a = jnp.concatenate([refs[k][...], refs[k + 1][...]], axis=1)
        bh = jnp.concatenate([hi[at[k]], hi[at[k + 1]]], axis=0)
        bl = jnp.concatenate([lo[at[k]], lo[at[k + 1]]], axis=0)
        term = split_dot(a, bh, bl)
        acc = term if acc is None else acc + term
    if last:
        outs[0][...] = acc[:, :256]
        outs[1][...] = acc[:, 256:]
    else:
        outs[0][...] = acc


def second_product(operand, blocks, acc=None, last=False):
    offsets = tuple(off for off, _ in blocks)
    rows, cols = blocks[0][1].shape
    args = list(operand) + [x for _, x in blocks] + ([] if acc is None else [acc])
    if last:
        shapes = (jax.ShapeDtypeStruct((rows, 2 * cols), F32),) * 2
    else:
        shapes = jax.ShapeDtypeStruct((rows, 4 * cols), F32)
    return pl.pallas_call(
        functools.partial(second_kernel, offsets, acc is not None, last),
        out_shape=shapes,
        in_specs=[VM] * len(args),
        out_specs=(VM, VM) if last else VM,
        compiler_params=PARAMS,
        cost_estimate=pl.CostEstimate(
            flops=len(offsets) * 3 * 2 * rows * cols * 4 * cols, bytes_accessed=0, transcendentals=0
        ),
    )(*args)


def join_kernel(own, both, mine, other):
    put_halves(own[...] + both[1 - lax.axis_index("c")], mine, other)


def join(own, give):
    both = lax.all_gather(give, "c", axis=0)
    rows, cols = own.shape
    block = jax.ShapeDtypeStruct((rows, cols // 2), F32)
    return pl.pallas_call(
        join_kernel,
        out_shape=(block, block),
        in_specs=[VM, VM],
        out_specs=(VM, VM),
        compiler_params=PARAMS,
    )(own, both)


def filter_kernel(final, kept, mine, pair, *refs):
    other = 1 - lax.axis_index("xl")
    lane = lax.broadcasted_iota(jnp.int32, (BS, 2 * BS), 1)
    for i in range(kept.shape[1]):
        strip = slice(i * BS, (i + 1) * BS)
        filt = jnp.where(lane < BS, kept[0, i], kept[1, i]).astype(F32)
        total = filt * (mine[strip, :] + pair[other, strip, :])
        if final:
            square = refs[0][strip, :]
            refs[1][strip, :] = square
            refs[2][strip, :] = 3.0 * square - 2.0 * total
        else:
            refs[0][strip, :] = total


def filtered(kept, halves, square=None):
    mine, other = halves
    final = square is not None
    pair = lax.all_gather(other, "xl", axis=0)
    args = [kept, mine, pair] + ([square] if final else [])
    block = jax.ShapeDtypeStruct(mine.shape, F32)
    return pl.pallas_call(
        functools.partial(filter_kernel, final),
        out_shape=(block, block) if final else block,
        in_specs=[SM] + [VM] * (len(args) - 1),
        out_specs=(VM, VM) if final else VM,
        compiler_params=PARAMS,
    )(*args)


def shift(x, axis, step):
    n = SIZES[AXES.index(axis)]
    return lax.ppermute(x, axis, [(i, (i + step) % n) for i in range(n)])


def together(*xs):
    return lax.optimization_barrier(xs)


def chain(x, axis, step, count):
    out = []
    for _ in range(count):
        x = shift(x, axis, step)
        out.append(x)
    return out


def body(density, atom_sizes, pattern, kept):
    pattern = pattern.T
    masked = pl.pallas_call(
        mask_kernel,
        out_shape=jax.ShapeDtypeStruct(density.shape, F32),
        in_specs=[HB] * 3,
        out_specs=VM,
        scratch_shapes=[
            pltpu.SMEM(atom_sizes.shape, jnp.int32),
            pltpu.SMEM(pattern.shape, jnp.int32),
            pltpu.VMEM(density.shape, F32),
            pltpu.SemaphoreType.DMA((3,)),
        ],
        compiler_params=WHOLE,
    )(atom_sizes, pattern, density)

    left = lax.all_gather(masked, ("z", "c"), axis=0)

    near = lax.ppermute(masked, ("xh", "xl"), [(0, 0), (1, 2), (2, 1), (3, 3)])
    far = lax.ppermute(masked, ("xh", "xl"), [(1, 0), (2, 3), (0, 2), (3, 1)])
    near_up, near_down = chain(near, "y", 1, 4), chain(near, "y", -1, 3)
    far_up, far_down = chain(far, "y", 1, 3), chain(far, "y", -1, 4)
    offsets = [0, -1, 1, -2, 2, -3, 3, 4]
    near = [near] + [x for pair in zip(near_up, near_down) for x in pair] + [near_up[3]]
    far = [far] + [x for pair in zip(far_up, far_down) for x in pair] + [far_down[3]]
    hi, lo, give = pack(offsets, near, far)
    took = shift(give, "c", 1)
    mine, other, took = together(*first_product(left, hi, lo), took)
    square = filtered(kept.T, (mine, other))

    operand = phase_rows(hi, lo, took)
    up, down = chain(square, "z", 1, 6), chain(square, "z", -1, 5)
    blocks = [(0, square)]
    for s in range(5):
        blocks += [(-s - 1, up[s]), (s + 1, down[s])]
    blocks.append((-6, up[5]))
    acc = second_product(operand, blocks[:4])
    acc = second_product(operand, blocks[4:8], acc)
    halves = join(*second_product(operand, blocks[8:], acc, last=True))
    return filtered(kept.T, halves, square)


def solution(mesh):
    fine = Mesh(mesh.devices.reshape(SIZES), AXES)
    placed = (P(ROW, COL), P(), P(ROW, COL), P(ROW, COL))
    return jax.shard_map(
        body,
        mesh=fine,
        in_specs=placed,
        out_specs=(P(ROW, COL), P(ROW, COL)),
        check_vma=False,
    )
```

```python
import functools

import jax
import jax.numpy as jnp
from jax import lax
from jax.experimental import pallas as pl
from jax.experimental.pallas import tpu as pltpu
from jax.sharding import Mesh, PartitionSpec as P

BS = 64
AXES = ("xh", "y", "xl", "z", "c")
SIZES = (2, 8, 2, 12, 2)
NY = 8
NZ = 12
ROW = ("xh", "y")
COL = ("xl", "z", "c")
F32 = jnp.float32
BF16 = jnp.bfloat16
VM = pl.BlockSpec(memory_space=pltpu.VMEM)
SM = pl.BlockSpec(memory_space=pltpu.SMEM)
HB = pl.BlockSpec(memory_space=pltpu.HBM)
PARAMS = pltpu.CompilerParams(vmem_limit_bytes=32 * 1024 * 1024)
WIDE = pltpu.CompilerParams(vmem_limit_bytes=50 * 1024 * 1024)
WHOLE = pltpu.CompilerParams(vmem_limit_bytes=64 * 1024 * 1024 - 128 * 1024)


def mask_kernel(sizes_hbm, pattern_hbm, density_hbm, out, sizes, pattern, density, sems):
    copies = [
        pltpu.make_async_copy(sizes_hbm, sizes, sems.at[0]),
        pltpu.make_async_copy(pattern_hbm, pattern, sems.at[1]),
        pltpu.make_async_copy(density_hbm, density, sems.at[2]),
    ]
    for copy in copies:
        copy.start()
    col_blocks, row_blocks = pattern.shape
    first_row = (lax.axis_index("xh") * NY + lax.axis_index("y")) * row_blocks
    first_col = ((lax.axis_index("xl") * NZ + lax.axis_index("z")) * 2 + lax.axis_index("c")) * col_blocks
    sub = lax.broadcasted_iota(jnp.int32, (BS, 2 * BS), 0)
    lane = lax.broadcasted_iota(jnp.int32, (BS, 2 * BS), 1)
    left = lane < BS
    for copy in copies:
        copy.wait()
    size_col = jnp.where(left, sizes[first_col], sizes[first_col + 1])
    valid_col = (jnp.where(left, lane, lane - BS) < size_col).astype(F32)
    for i in range(row_blocks):
        stored = jnp.where(left, pattern[0, i], pattern[1, i]).astype(F32)
        valid = (sub < sizes[first_row + i]).astype(F32) * valid_col * stored
        out[i * BS : (i + 1) * BS, :] = density[i * BS : (i + 1) * BS, :] * valid


def split(x):
    hi = x.astype(BF16)
    return hi, (x - hi.astype(F32)).astype(BF16)


dot = functools.partial(jnp.dot, preferred_element_type=F32)


def split_dot(a, bh, bl):
    ah, al = split(a)
    return dot(ah, bh) + (dot(ah, bl) + dot(al, bh))


def put_halves(total, mine, other):
    same = lax.axis_index("xl") == lax.axis_index("xh")
    near, far = total[:, :128], total[:, 128:]
    mine[...] = jnp.where(same, near, far)
    other[...] = jnp.where(same, far, near)


def pack_kernel(offsets, *refs):
    n = len(offsets)
    near, far = refs[:n], refs[n : 2 * n]
    hi, lo, give = refs[2 * n :]
    y = lax.axis_index("y")
    c = lax.axis_index("c")
    for k, off in enumerate(offsets):
        first = 3 * lax.rem(y + (off + NY), NY)
        for t in range(3):
            rows = slice(t * 128, (t + 1) * 128)
            unit = jnp.concatenate([near[k][rows, :], far[k][rows, :]], axis=1)
            hi[first + t], lo[first + t] = split(unit)

            @pl.when(lax.rem(first + t, 2) != c)
            def _():
                give[(first + t) // 2] = unit


def pack(offsets, near, far):
    rows, cols = near[0].shape
    args = near + far
    half = jax.ShapeDtypeStruct((2 * NZ, 128, 2 * cols), BF16)
    return pl.pallas_call(
        functools.partial(pack_kernel, tuple(offsets)),
        out_shape=(half, half, jax.ShapeDtypeStruct((NZ, 128, 2 * cols), F32)),
        in_specs=[VM] * len(args),
        out_specs=(VM,) * 3,
        compiler_params=PARAMS,
    )(*args)


def rows_kernel(hi, lo, took, rows_hi, rows_lo):
    c = lax.axis_index("c")
    for z in range(NZ):
        rows_hi[z, :, :256] = hi[2 * z + c]
        rows_lo[z, :, :256] = lo[2 * z + c]
        rows_hi[z, :, 256:], rows_lo[z, :, 256:] = split(took[z])


def phase_rows(hi, lo, took):
    units, depth, cols = took.shape
    half = jax.ShapeDtypeStruct((units, depth, 2 * cols), BF16)
    return pl.pallas_call(
        rows_kernel,
        out_shape=(half, half),
        in_specs=[VM] * 3,
        out_specs=(VM, VM),
        compiler_params=PARAMS,
    )(hi, lo, took)


def first_kernel(left, hi, lo, mine, other, held, sems):
    parts, per = held.shape[:2]
    copies = [
        pltpu.make_async_copy(left.at[pl.ds(per * p, per)], held.at[p], sems.at[p]) for p in range(parts)
    ]
    for copy in copies:
        copy.start()
    for copy in copies:
        copy.wait()
    acc = None
    for z in range(NZ):
        u = 2 * z
        p, k = divmod(u, per)
        a = jnp.concatenate([held[p, k], held[p, k + 1]], axis=1)
        bh = jnp.concatenate([hi[u], hi[u + 1]], axis=0)
        bl = jnp.concatenate([lo[u], lo[u + 1]], axis=0)
        term = split_dot(a, bh, bl)
        acc = term if acc is None else acc + term
    put_halves(acc, mine, other)


def first_product(left, hi, lo):
    units, rows, cols = left.shape
    parts = 6
    block = jax.ShapeDtypeStruct((rows, cols), F32)
    return pl.pallas_call(
        first_kernel,
        out_shape=(block, block),
        in_specs=[HB, VM, VM],
        out_specs=(VM, VM),
        scratch_shapes=[
            pltpu.VMEM((parts, units // parts, rows, cols), F32),
            pltpu.SemaphoreType.DMA((parts,)),
        ],
        compiler_params=WIDE,
        cost_estimate=pl.CostEstimate(
            flops=NZ * 3 * 2 * rows * 2 * cols * 2 * cols, bytes_accessed=0, transcendentals=0
        ),
    )(left, hi, lo)


def second_kernel(offsets, hi, lo, *refs):
    blocks, (own, give) = refs[:-2], refs[-2:]
    z = lax.axis_index("z")
    at = [lax.rem(z + (off + NZ), NZ) for off in offsets]
    acc = None
    for k in range(0, len(offsets), 2):
        pair = range(k, min(k + 2, len(offsets)))
        a = jnp.concatenate([blocks[i][...] for i in pair], axis=1)
        bh = jnp.concatenate([hi[at[i]] for i in pair], axis=0)
        bl = jnp.concatenate([lo[at[i]] for i in pair], axis=0)
        term = split_dot(a, bh, bl)
        acc = term if acc is None else acc + term
    own[...] = acc[:, :256]
    give[...] = acc[:, 256:]


def second_product(operand, blocks):
    offsets = tuple(off for off, _ in blocks)
    rows, cols = blocks[0][1].shape
    args = list(operand) + [x for _, x in blocks]
    return pl.pallas_call(
        functools.partial(second_kernel, offsets),
        out_shape=(jax.ShapeDtypeStruct((rows, 2 * cols), F32),) * 2,
        in_specs=[VM] * len(args),
        out_specs=(VM, VM),
        compiler_params=PARAMS,
        cost_estimate=pl.CostEstimate(
            flops=len(offsets) * 3 * 2 * rows * cols * 4 * cols, bytes_accessed=0, transcendentals=0
        ),
    )(*args)


def join_kernel(hi, lo, own, both, near_block, far_block, mine, other):
    c = lax.axis_index("c")
    u = 2 * lax.rem(lax.axis_index("z") + NZ // 2, NZ)
    a = jnp.concatenate([near_block[...], far_block[...]], axis=1)
    bh = jnp.concatenate([hi[u + c], hi[u + 1 - c]], axis=0)
    bl = jnp.concatenate([lo[u + c], lo[u + 1 - c]], axis=0)
    put_halves(own[...] + both[1 - c] + split_dot(a, bh, bl), mine, other)


def join(hi, lo, own, give, last, last_sib):
    both = lax.all_gather(give, "c", axis=0)
    args = (hi, lo, own, both, last, last_sib)
    block = jax.ShapeDtypeStruct(last.shape, F32)
    return pl.pallas_call(
        join_kernel,
        out_shape=(block, block),
        in_specs=[VM] * len(args),
        out_specs=(VM, VM),
        compiler_params=PARAMS,
    )(*args)


def filter_kernel(final, kept, mine, pair, *refs):
    other = 1 - lax.axis_index("xl")
    lane = lax.broadcasted_iota(jnp.int32, (BS, 2 * BS), 1)
    for i in range(kept.shape[1]):
        strip = slice(i * BS, (i + 1) * BS)
        filt = jnp.where(lane < BS, kept[0, i], kept[1, i]).astype(F32)
        total = filt * (mine[strip, :] + pair[other, strip, :])
        if final:
            square = refs[0][strip, :]
            refs[1][strip, :] = square
            refs[2][strip, :] = 3.0 * square - 2.0 * total
        else:
            refs[0][strip, :] = total


def filtered(kept, halves, square=None):
    mine, other = halves
    final = square is not None
    pair = lax.all_gather(other, "xl", axis=0)
    args = [kept, mine, pair] + ([square] if final else [])
    block = jax.ShapeDtypeStruct(mine.shape, F32)
    return pl.pallas_call(
        functools.partial(filter_kernel, final),
        out_shape=(block, block) if final else block,
        in_specs=[SM] + [VM] * (len(args) - 1),
        out_specs=(VM, VM) if final else VM,
        compiler_params=PARAMS,
    )(*args)


def shift(x, axis, step):
    n = SIZES[AXES.index(axis)]
    return lax.ppermute(x, axis, [(i, (i + step) % n) for i in range(n)])


def together(*xs):
    return lax.optimization_barrier(xs)


def chain(x, axis, step, count):
    out = []
    for _ in range(count):
        x = shift(x, axis, step)
        out.append(x)
    return out


def body(density, atom_sizes, pattern, kept):
    pattern = pattern.T
    masked = pl.pallas_call(
        mask_kernel,
        out_shape=jax.ShapeDtypeStruct(density.shape, F32),
        in_specs=[HB] * 3,
        out_specs=VM,
        scratch_shapes=[
            pltpu.SMEM(atom_sizes.shape, jnp.int32),
            pltpu.SMEM(pattern.shape, jnp.int32),
            pltpu.VMEM(density.shape, F32),
            pltpu.SemaphoreType.DMA((3,)),
        ],
        compiler_params=WHOLE,
    )(atom_sizes, pattern, density)

    left = lax.all_gather(masked, ("z", "c"), axis=0)

    near = lax.ppermute(masked, ("xh", "xl"), [(0, 0), (1, 2), (2, 1), (3, 3)])
    far = lax.ppermute(masked, ("xh", "xl"), [(1, 0), (2, 3), (0, 2), (3, 1)])
    near_up, near_down = chain(near, "y", 1, 4), chain(near, "y", -1, 3)
    far_up, far_down = chain(far, "y", 1, 3), chain(far, "y", -1, 4)
    offsets = [0, -1, 1, -2, 2, -3, 3, 4]
    near = [near] + [x for pair in zip(near_up, near_down) for x in pair] + [near_up[3]]
    far = [far] + [x for pair in zip(far_up, far_down) for x in pair] + [far_down[3]]
    hi, lo, give = pack(offsets, near, far)
    took = shift(give, "c", 1)
    mine, other, took = together(*first_product(left, hi, lo), took)
    square = filtered(kept.T, (mine, other))

    down = chain(square, "z", -1, 1)
    down[0], operand = together(down[0], phase_rows(hi, lo, took))
    down += chain(down[0], "z", -1, 4)
    up = chain(square, "z", 1, 6)
    crossed = [(2 * z + c, 2 * ((z - 1) % NZ) + 1 - c) for z in range(NZ) for c in range(2)]
    last_sib = lax.ppermute(down[4], ("z", "c"), crossed)
    blocks = [(0, square)]
    for s in range(5):
        blocks += [(-s - 1, up[s]), (s + 1, down[s])]
    halves = join(hi, lo, *second_product(operand, blocks), up[5], last_sib)
    return filtered(kept.T, halves, square)


def solution(mesh):
    fine = Mesh(mesh.devices.reshape(SIZES), AXES)
    placed = (P(ROW, COL), P(), P(ROW, COL), P(ROW, COL))
    return jax.shard_map(
        body,
        mesh=fine,
        in_specs=placed,
        out_specs=(P(ROW, COL), P(ROW, COL)),
        check_vma=False,
    )
```

```python
import functools

import jax
import jax.numpy as jnp
from jax import lax
from jax.experimental import pallas as pl
from jax.experimental.pallas import tpu as pltpu
from jax.sharding import Mesh, PartitionSpec as P

BS = 64
AXES = ("xh", "y", "xl", "z", "c")
SIZES = (2, 8, 2, 12, 2)
NY = 8
NZ = 12
ROW = ("xh", "y")
COL = ("xl", "z", "c")
F32 = jnp.float32
BF16 = jnp.bfloat16
VM = pl.BlockSpec(memory_space=pltpu.VMEM)
SM = pl.BlockSpec(memory_space=pltpu.SMEM)
HB = pl.BlockSpec(memory_space=pltpu.HBM)
PARAMS = pltpu.CompilerParams(vmem_limit_bytes=32 * 1024 * 1024)
WIDE = pltpu.CompilerParams(vmem_limit_bytes=50 * 1024 * 1024)
WHOLE = pltpu.CompilerParams(vmem_limit_bytes=64 * 1024 * 1024 - 128 * 1024)


def mask_kernel(sizes_hbm, pattern_hbm, density_hbm, out, sizes, pattern, density, sems):
    copies = [
        pltpu.make_async_copy(sizes_hbm, sizes, sems.at[0]),
        pltpu.make_async_copy(pattern_hbm, pattern, sems.at[1]),
        pltpu.make_async_copy(density_hbm, density, sems.at[2]),
    ]
    for copy in copies:
        copy.start()
    col_blocks, row_blocks = pattern.shape
    first_row = (lax.axis_index("xh") * NY + lax.axis_index("y")) * row_blocks
    first_col = ((lax.axis_index("xl") * NZ + lax.axis_index("z")) * 2 + lax.axis_index("c")) * col_blocks
    sub = lax.broadcasted_iota(jnp.int32, (BS, 2 * BS), 0)
    lane = lax.broadcasted_iota(jnp.int32, (BS, 2 * BS), 1)
    left = lane < BS
    for copy in copies:
        copy.wait()
    size_col = jnp.where(left, sizes[first_col], sizes[first_col + 1])
    valid_col = (jnp.where(left, lane, lane - BS) < size_col).astype(F32)
    for i in range(row_blocks):
        stored = jnp.where(left, pattern[0, i], pattern[1, i]).astype(F32)
        valid = (sub < sizes[first_row + i]).astype(F32) * valid_col * stored
        out[i * BS : (i + 1) * BS, :] = density[i * BS : (i + 1) * BS, :] * valid


def split(x):
    hi = x.astype(BF16)
    return hi, (x - hi.astype(F32)).astype(BF16)


dot = functools.partial(jnp.dot, preferred_element_type=F32)


def split_dot(a, bh, bl):
    ah, al = split(a)
    return dot(ah, bh) + (dot(ah, bl) + dot(al, bh))


def put_halves(total, mine, other):
    same = lax.axis_index("xl") == lax.axis_index("xh")
    near, far = total[:, :128], total[:, 128:]
    mine[...] = jnp.where(same, near, far)
    other[...] = jnp.where(same, far, near)


def pack_kernel(offsets, *refs):
    n = len(offsets)
    near, far = refs[:n], refs[n : 2 * n]
    hi, lo, give = refs[2 * n :]
    y = lax.axis_index("y")
    c = lax.axis_index("c")
    for k, off in enumerate(offsets):
        first = 3 * lax.rem(y + (off + NY), NY)
        for t in range(3):
            rows = slice(t * 128, (t + 1) * 128)
            unit = jnp.concatenate([near[k][rows, :], far[k][rows, :]], axis=1)
            hi[first + t], lo[first + t] = split(unit)

            @pl.when(lax.rem(first + t, 2) != c)
            def _():
                give[(first + t) // 2] = unit


def pack(offsets, near, far):
    rows, cols = near[0].shape
    args = near + far
    half = jax.ShapeDtypeStruct((2 * NZ, 128, 2 * cols), BF16)
    return pl.pallas_call(
        functools.partial(pack_kernel, tuple(offsets)),
        out_shape=(half, half, jax.ShapeDtypeStruct((NZ, 128, 2 * cols), F32)),
        in_specs=[VM] * len(args),
        out_specs=(VM,) * 3,
        compiler_params=PARAMS,
    )(*args)


def rows_kernel(hi, lo, took, rows_hi, rows_lo):
    c = lax.axis_index("c")
    for z in range(NZ):
        rows_hi[z, :, :256] = hi[2 * z + c]
        rows_lo[z, :, :256] = lo[2 * z + c]
        rows_hi[z, :, 256:], rows_lo[z, :, 256:] = split(took[z])


def phase_rows(hi, lo, took):
    units, depth, cols = took.shape
    half = jax.ShapeDtypeStruct((units, depth, 2 * cols), BF16)
    return pl.pallas_call(
        rows_kernel,
        out_shape=(half, half),
        in_specs=[VM] * 3,
        out_specs=(VM, VM),
        compiler_params=PARAMS,
    )(hi, lo, took)


def first_kernel(left, hi, lo, mine, other, held, sems):
    parts, per = held.shape[:2]
    copies = [
        pltpu.make_async_copy(left.at[pl.ds(per * p, per)], held.at[p], sems.at[p]) for p in range(parts)
    ]
    for copy in copies:
        copy.start()
    for copy in copies:
        copy.wait()
    acc = None
    for z in range(NZ):
        u = 2 * z
        p, k = divmod(u, per)
        a = jnp.concatenate([held[p, k], held[p, k + 1]], axis=1)
        bh = jnp.concatenate([hi[u], hi[u + 1]], axis=0)
        bl = jnp.concatenate([lo[u], lo[u + 1]], axis=0)
        term = split_dot(a, bh, bl)
        acc = term if acc is None else acc + term
    put_halves(acc, mine, other)


def first_product(left, hi, lo):
    units, rows, cols = left.shape
    parts = 6
    block = jax.ShapeDtypeStruct((rows, cols), F32)
    return pl.pallas_call(
        first_kernel,
        out_shape=(block, block),
        in_specs=[HB, VM, VM],
        out_specs=(VM, VM),
        scratch_shapes=[
            pltpu.VMEM((parts, units // parts, rows, cols), F32),
            pltpu.SemaphoreType.DMA((parts,)),
        ],
        compiler_params=WIDE,
        cost_estimate=pl.CostEstimate(
            flops=NZ * 3 * 2 * rows * 2 * cols * 2 * cols, bytes_accessed=0, transcendentals=0
        ),
    )(left, hi, lo)


def second_kernel(offsets, has_acc, last, hi, lo, *refs):
    n = len(offsets)
    acc = refs[n][...] if has_acc else None
    outs = refs[n + has_acc :]
    z = lax.axis_index("z")
    sign = 1 - 2 * lax.rem(z + lax.axis_index("c"), 2)
    at = [lax.rem(z + sign * off + NZ, NZ) for off in offsets]
    for k in range(0, n, 2):
        a = jnp.concatenate([refs[k][...], refs[k + 1][...]], axis=1)
        bh = jnp.concatenate([hi[at[k]], hi[at[k + 1]]], axis=0)
        bl = jnp.concatenate([lo[at[k]], lo[at[k + 1]]], axis=0)
        term = split_dot(a, bh, bl)
        acc = term if acc is None else acc + term
    if last:
        outs[0][...] = acc[:, :256]
        outs[1][...] = acc[:, 256:]
    else:
        outs[0][...] = acc


def second_product(operand, blocks, acc=None, last=False):
    offsets = tuple(off for off, _ in blocks)
    rows, cols = blocks[0][1].shape
    args = list(operand) + [x for _, x in blocks] + ([] if acc is None else [acc])
    if last:
        shapes = (jax.ShapeDtypeStruct((rows, 2 * cols), F32),) * 2
    else:
        shapes = jax.ShapeDtypeStruct((rows, 4 * cols), F32)
    return pl.pallas_call(
        functools.partial(second_kernel, offsets, acc is not None, last),
        out_shape=shapes,
        in_specs=[VM] * len(args),
        out_specs=(VM, VM) if last else VM,
        compiler_params=PARAMS,
        cost_estimate=pl.CostEstimate(
            flops=len(offsets) * 3 * 2 * rows * cols * 4 * cols, bytes_accessed=0, transcendentals=0
        ),
    )(*args)


def join_kernel(own, both, mine, other):
    put_halves(own[...] + both[1 - lax.axis_index("c")], mine, other)


def join(own, give):
    both = lax.all_gather(give, "c", axis=0)
    rows, cols = own.shape
    block = jax.ShapeDtypeStruct((rows, cols // 2), F32)
    return pl.pallas_call(
        join_kernel,
        out_shape=(block, block),
        in_specs=[VM, VM],
        out_specs=(VM, VM),
        compiler_params=PARAMS,
    )(own, both)


def filter_kernel(final, kept, mine, pair, *refs):
    other = 1 - lax.axis_index("xl")
    lane = lax.broadcasted_iota(jnp.int32, (BS, 2 * BS), 1)
    for i in range(kept.shape[1]):
        strip = slice(i * BS, (i + 1) * BS)
        filt = jnp.where(lane < BS, kept[0, i], kept[1, i]).astype(F32)
        total = filt * (mine[strip, :] + pair[other, strip, :])
        if final:
            square = refs[0][strip, :]
            refs[1][strip, :] = square
            refs[2][strip, :] = 3.0 * square - 2.0 * total
        else:
            refs[0][strip, :] = total


def filtered(kept, halves, square=None):
    mine, other = halves
    final = square is not None
    pair = lax.all_gather(other, "xl", axis=0)
    args = [kept, mine, pair] + ([square] if final else [])
    block = jax.ShapeDtypeStruct(mine.shape, F32)
    return pl.pallas_call(
        functools.partial(filter_kernel, final),
        out_shape=(block, block) if final else block,
        in_specs=[SM] + [VM] * (len(args) - 1),
        out_specs=(VM, VM) if final else VM,
        compiler_params=PARAMS,
    )(*args)


def shift(x, axis, step):
    n = SIZES[AXES.index(axis)]
    return lax.ppermute(x, axis, [(i, (i + step) % n) for i in range(n)])


def together(*xs):
    return lax.optimization_barrier(xs)


def chain(x, axis, step, count):
    out = []
    for _ in range(count):
        x = shift(x, axis, step)
        out.append(x)
    return out


def swaps(x, first, count):
    out = []
    for s in range(count):
        pairs = []
        for z in range(NZ):
            for c in range(2):
                to = z + 1 if (z + first + s + c) % 2 == 0 else z - 1
                pairs.append((2 * z + c, 2 * (to % NZ) + c))
        x = lax.ppermute(x, ("z", "c"), pairs)
        out.append(x)
    return out


def body(density, atom_sizes, pattern, kept):
    pattern = pattern.T
    masked = pl.pallas_call(
        mask_kernel,
        out_shape=jax.ShapeDtypeStruct(density.shape, F32),
        in_specs=[HB] * 3,
        out_specs=VM,
        scratch_shapes=[
            pltpu.SMEM(atom_sizes.shape, jnp.int32),
            pltpu.SMEM(pattern.shape, jnp.int32),
            pltpu.VMEM(density.shape, F32),
            pltpu.SemaphoreType.DMA((3,)),
        ],
        compiler_params=WHOLE,
    )(atom_sizes, pattern, density)

    left = lax.all_gather(masked, ("z", "c"), axis=0)

    near = lax.ppermute(masked, ("xh", "xl"), [(0, 0), (1, 2), (2, 1), (3, 3)])
    far = lax.ppermute(masked, ("xh", "xl"), [(1, 0), (2, 3), (0, 2), (3, 1)])
    near_up, near_down = chain(near, "y", 1, 4), chain(near, "y", -1, 3)
    far_up, far_down = chain(far, "y", 1, 3), chain(far, "y", -1, 4)
    offsets = [0, -1, 1, -2, 2, -3, 3, 4]
    near = [near] + [x for pair in zip(near_up, near_down) for x in pair] + [near_up[3]]
    far = [far] + [x for pair in zip(far_up, far_down) for x in pair] + [far_down[3]]
    hi, lo, give = pack(offsets, near, far)
    took = shift(give, "c", 1)
    mine, other, took = together(*first_product(left, hi, lo), took)
    square = filtered(kept.T, (mine, other))

    operand = phase_rows(hi, lo, took)
    ahead, back = swaps(square, 0, 6), swaps(square, 1, 5)
    blocks = [(0, square)]
    for s in range(5):
        off = s + 1 if s % 2 == 0 else -s - 1
        blocks += [(off, ahead[s]), (-off, back[s])]
    blocks.append((-6, ahead[5]))
    acc = second_product(operand, blocks[:4])
    acc = second_product(operand, blocks[4:8], acc)
    halves = join(*second_product(operand, blocks[8:], acc, last=True))
    return filtered(kept.T, halves, square)


def solution(mesh):
    fine = Mesh(mesh.devices.reshape(SIZES), AXES)
    placed = (P(ROW, COL), P(), P(ROW, COL), P(ROW, COL))
    return jax.shard_map(
        body,
        mesh=fine,
        in_specs=placed,
        out_specs=(P(ROW, COL), P(ROW, COL)),
        check_vma=False,
    )
```

```python
import functools

import jax
import jax.numpy as jnp
from jax import lax
from jax.experimental import pallas as pl
from jax.experimental.pallas import tpu as pltpu
from jax.sharding import Mesh, PartitionSpec as P

BS = 64
AXES = ("xh", "y", "xl", "z", "c")
SIZES = (2, 8, 2, 12, 2)
NY = 8
NZ = 12
ROW = ("xh", "y")
COL = ("xl", "z", "c")
F32 = jnp.float32
BF16 = jnp.bfloat16
VM = pl.BlockSpec(memory_space=pltpu.VMEM)
SM = pl.BlockSpec(memory_space=pltpu.SMEM)
HB = pl.BlockSpec(memory_space=pltpu.HBM)
PARAMS = pltpu.CompilerParams(vmem_limit_bytes=32 * 1024 * 1024)
WIDE = pltpu.CompilerParams(vmem_limit_bytes=50 * 1024 * 1024)
WHOLE = pltpu.CompilerParams(vmem_limit_bytes=64 * 1024 * 1024 - 128 * 1024)


def mask_kernel(sizes_hbm, pattern_hbm, density_hbm, out, sizes, pattern, density, sems):
    copies = [
        pltpu.make_async_copy(sizes_hbm, sizes, sems.at[0]),
        pltpu.make_async_copy(pattern_hbm, pattern, sems.at[1]),
        pltpu.make_async_copy(density_hbm, density, sems.at[2]),
    ]
    for copy in copies:
        copy.start()
    col_blocks, row_blocks = pattern.shape
    first_row = (lax.axis_index("xh") * NY + lax.axis_index("y")) * row_blocks
    first_col = ((lax.axis_index("xl") * NZ + lax.axis_index("z")) * 2 + lax.axis_index("c")) * col_blocks
    sub = lax.broadcasted_iota(jnp.int32, (BS, 2 * BS), 0)
    lane = lax.broadcasted_iota(jnp.int32, (BS, 2 * BS), 1)
    left = lane < BS
    for copy in copies:
        copy.wait()
    size_col = jnp.where(left, sizes[first_col], sizes[first_col + 1])
    valid_col = (jnp.where(left, lane, lane - BS) < size_col).astype(F32)
    for i in range(row_blocks):
        stored = jnp.where(left, pattern[0, i], pattern[1, i]).astype(F32)
        valid = (sub < sizes[first_row + i]).astype(F32) * valid_col * stored
        out[i * BS : (i + 1) * BS, :] = density[i * BS : (i + 1) * BS, :] * valid


def split(x):
    hi = x.astype(BF16)
    return hi, (x - hi.astype(F32)).astype(BF16)


dot = functools.partial(jnp.dot, preferred_element_type=F32)


def split_dot(a, bh, bl):
    ah, al = split(a)
    return dot(ah, bh) + (dot(ah, bl) + dot(al, bh))


def put_halves(total, mine, other):
    same = lax.axis_index("xl") == lax.axis_index("xh")
    near, far = total[:, :128], total[:, 128:]
    mine[...] = jnp.where(same, near, far)
    other[...] = jnp.where(same, far, near)


def pack_kernel(offsets, *refs):
    n = len(offsets)
    near, far = refs[:n], refs[n : 2 * n]
    hi, lo, give = refs[2 * n :]
    y = lax.axis_index("y")
    c = lax.axis_index("c")
    for k, off in enumerate(offsets):
        first = 3 * lax.rem(y + (off + NY), NY)
        for t in range(3):
            rows = slice(t * 128, (t + 1) * 128)
            unit = jnp.concatenate([near[k][rows, :], far[k][rows, :]], axis=1)
            hi[first + t], lo[first + t] = split(unit)

            @pl.when(lax.rem(first + t, 2) != c)
            def _():
                give[(first + t) // 2] = unit


def pack(offsets, near, far):
    rows, cols = near[0].shape
    args = near + far
    half = jax.ShapeDtypeStruct((2 * NZ, 128, 2 * cols), BF16)
    return pl.pallas_call(
        functools.partial(pack_kernel, tuple(offsets)),
        out_shape=(half, half, jax.ShapeDtypeStruct((NZ, 128, 2 * cols), F32)),
        in_specs=[VM] * len(args),
        out_specs=(VM,) * 3,
        compiler_params=PARAMS,
    )(*args)


def rows_kernel(hi, lo, took, rows_hi, rows_lo):
    c = lax.axis_index("c")
    for z in range(NZ):
        rows_hi[z, :, :256] = hi[2 * z + c]
        rows_lo[z, :, :256] = lo[2 * z + c]
        rows_hi[z, :, 256:], rows_lo[z, :, 256:] = split(took[z])


def phase_rows(hi, lo, took):
    units, depth, cols = took.shape
    half = jax.ShapeDtypeStruct((units, depth, 2 * cols), BF16)
    return pl.pallas_call(
        rows_kernel,
        out_shape=(half, half),
        in_specs=[VM] * 3,
        out_specs=(VM, VM),
        compiler_params=PARAMS,
    )(hi, lo, took)


def first_kernel(left, hi, lo, mine, other, held, sems):
    parts, per = held.shape[:2]
    copies = [
        pltpu.make_async_copy(left.at[pl.ds(per * p, per)], held.at[p], sems.at[p]) for p in range(parts)
    ]
    for copy in copies:
        copy.start()
    for copy in copies:
        copy.wait()
    acc = None
    for z in range(NZ):
        u = 2 * z
        p, k = divmod(u, per)
        a = jnp.concatenate([held[p, k], held[p, k + 1]], axis=1)
        bh = jnp.concatenate([hi[u], hi[u + 1]], axis=0)
        bl = jnp.concatenate([lo[u], lo[u + 1]], axis=0)
        term = split_dot(a, bh, bl)
        acc = term if acc is None else acc + term
    put_halves(acc, mine, other)


def first_product(left, hi, lo):
    units, rows, cols = left.shape
    parts = 6
    block = jax.ShapeDtypeStruct((rows, cols), F32)
    return pl.pallas_call(
        first_kernel,
        out_shape=(block, block),
        in_specs=[HB, VM, VM],
        out_specs=(VM, VM),
        scratch_shapes=[
            pltpu.VMEM((parts, units // parts, rows, cols), F32),
            pltpu.SemaphoreType.DMA((parts,)),
        ],
        compiler_params=WIDE,
        cost_estimate=pl.CostEstimate(
            flops=NZ * 3 * 2 * rows * 2 * cols * 2 * cols, bytes_accessed=0, transcendentals=0
        ),
    )(left, hi, lo)


def second_kernel(offsets, has_acc, last, hi, lo, *refs):
    n = len(offsets)
    acc = refs[n][...] if has_acc else None
    outs = refs[n + has_acc :]
    z = lax.axis_index("z")
    at = [lax.rem(z + (off + NZ), NZ) for off in offsets]
    for k in range(0, n, 2):
        a = jnp.concatenate([refs[k][...], refs[k + 1][...]], axis=1)
        bh = jnp.concatenate([hi[at[k]], hi[at[k + 1]]], axis=0)
        bl = jnp.concatenate([lo[at[k]], lo[at[k + 1]]], axis=0)
        term = split_dot(a, bh, bl)
        acc = term if acc is None else acc + term
    if last:
        outs[0][...] = acc[:, :256]
        outs[1][...] = acc[:, 256:]
    else:
        outs[0][...] = acc


def second_product(operand, blocks, acc=None, last=False):
    offsets = tuple(off for off, _ in blocks)
    rows, cols = blocks[0][1].shape
    args = list(operand) + [x for _, x in blocks] + ([] if acc is None else [acc])
    if last:
        shapes = (jax.ShapeDtypeStruct((rows, 2 * cols), F32),) * 2
    else:
        shapes = jax.ShapeDtypeStruct((rows, 4 * cols), F32)
    return pl.pallas_call(
        functools.partial(second_kernel, offsets, acc is not None, last),
        out_shape=shapes,
        in_specs=[VM] * len(args),
        out_specs=(VM, VM) if last else VM,
        compiler_params=PARAMS,
        cost_estimate=pl.CostEstimate(
            flops=len(offsets) * 3 * 2 * rows * cols * 4 * cols, bytes_accessed=0, transcendentals=0
        ),
    )(*args)


def join_kernel(own, both, mine, other):
    put_halves(own[...] + both[1 - lax.axis_index("c")], mine, other)


def join(own, give):
    both = lax.all_gather(give, "c", axis=0)
    rows, cols = own.shape
    block = jax.ShapeDtypeStruct((rows, cols // 2), F32)
    return pl.pallas_call(
        join_kernel,
        out_shape=(block, block),
        in_specs=[VM, VM],
        out_specs=(VM, VM),
        compiler_params=PARAMS,
    )(own, both)


def filter_kernel(final, kept, mine, pair, *refs):
    other = 1 - lax.axis_index("xl")
    lane = lax.broadcasted_iota(jnp.int32, (BS, 2 * BS), 1)
    for i in range(kept.shape[1]):
        strip = slice(i * BS, (i + 1) * BS)
        filt = jnp.where(lane < BS, kept[0, i], kept[1, i]).astype(F32)
        total = filt * (mine[strip, :] + pair[other, strip, :])
        if final:
            square = refs[0][strip, :]
            refs[1][strip, :] = square
            refs[2][strip, :] = 3.0 * square - 2.0 * total
        else:
            refs[0][strip, :] = total


def filtered(kept, halves, square=None):
    mine, other = halves
    final = square is not None
    pair = lax.all_gather(other, "xl", axis=0)
    args = [kept, mine, pair] + ([square] if final else [])
    block = jax.ShapeDtypeStruct(mine.shape, F32)
    return pl.pallas_call(
        functools.partial(filter_kernel, final),
        out_shape=(block, block) if final else block,
        in_specs=[SM] + [VM] * (len(args) - 1),
        out_specs=(VM, VM) if final else VM,
        compiler_params=PARAMS,
    )(*args)


def shift(x, axis, step):
    n = SIZES[AXES.index(axis)]
    return lax.ppermute(x, axis, [(i, (i + step) % n) for i in range(n)])


def together(*xs):
    return lax.optimization_barrier(xs)


def chain(x, axis, step, count):
    out = []
    for _ in range(count):
        x = shift(x, axis, step)
        out.append(x)
    return out


def body(density, atom_sizes, pattern, kept):
    pattern = pattern.T
    masked = pl.pallas_call(
        mask_kernel,
        out_shape=jax.ShapeDtypeStruct(density.shape, F32),
        in_specs=[HB] * 3,
        out_specs=VM,
        scratch_shapes=[
            pltpu.SMEM(atom_sizes.shape, jnp.int32),
            pltpu.SMEM(pattern.shape, jnp.int32),
            pltpu.VMEM(density.shape, F32),
            pltpu.SemaphoreType.DMA((3,)),
        ],
        compiler_params=WHOLE,
    )(atom_sizes, pattern, density)

    left = lax.all_gather(masked, ("z", "c"), axis=0)

    near = lax.ppermute(masked, ("xh", "xl"), [(0, 0), (1, 2), (2, 1), (3, 3)])
    far = lax.ppermute(masked, ("xh", "xl"), [(1, 0), (2, 3), (0, 2), (3, 1)])
    near_up, near_down = chain(near, "y", 1, 4), chain(near, "y", -1, 3)
    far_up, far_down = chain(far, "y", 1, 3), chain(far, "y", -1, 4)
    offsets = [0, -1, 1, -2, 2, -3, 3, 4]
    near = [near] + [x for pair in zip(near_up, near_down) for x in pair] + [near_up[3]]
    far = [far] + [x for pair in zip(far_up, far_down) for x in pair] + [far_down[3]]
    hi, lo, give = pack(offsets, near, far)
    took = shift(give, "c", 1)
    mine, other, took = together(*first_product(left, hi, lo), took)
    square = filtered(kept.T, (mine, other))

    operand = phase_rows(hi, lo, took)
    away = shift(square, "z", 6)
    up, down = chain(square, "z", 1, 4), chain(square, "z", -1, 4)
    blocks = [(0, square)]
    for s in range(3):
        blocks += [(-s - 1, up[s]), (s + 1, down[s])]
    blocks += [(6, away), (-4, up[3]), (4, down[3]), (5, shift(away, "z", 1)), (-5, shift(away, "z", -1))]
    acc = second_product(operand, blocks[:4])
    acc = second_product(operand, blocks[4:8], acc)
    halves = join(*second_product(operand, blocks[8:], acc, last=True))
    return filtered(kept.T, halves, square)


def solution(mesh):
    fine = Mesh(mesh.devices.reshape(SIZES), AXES)
    placed = (P(ROW, COL), P(), P(ROW, COL), P(ROW, COL))
    return jax.shard_map(
        body,
        mesh=fine,
        in_specs=placed,
        out_specs=(P(ROW, COL), P(ROW, COL)),
        check_vma=False,
    )
```

```python
import functools

import jax
import jax.numpy as jnp
from jax import lax
from jax.experimental import pallas as pl
from jax.experimental.pallas import tpu as pltpu
from jax.sharding import Mesh, PartitionSpec as P

BS = 64
AXES = ("xh", "y", "xl", "z", "c")
SIZES = (2, 8, 2, 12, 2)
NY = 8
NZ = 12
ROW = ("xh", "y")
COL = ("xl", "z", "c")
F32 = jnp.float32
BF16 = jnp.bfloat16
VM = pl.BlockSpec(memory_space=pltpu.VMEM)
SM = pl.BlockSpec(memory_space=pltpu.SMEM)
HB = pl.BlockSpec(memory_space=pltpu.HBM)
PARAMS = pltpu.CompilerParams(vmem_limit_bytes=32 * 1024 * 1024)
WIDE = pltpu.CompilerParams(vmem_limit_bytes=50 * 1024 * 1024)
WHOLE = pltpu.CompilerParams(vmem_limit_bytes=64 * 1024 * 1024 - 128 * 1024)


def mask_kernel(sizes_hbm, pattern_hbm, density_hbm, out, sizes, pattern, density, sems):
    copies = [
        pltpu.make_async_copy(sizes_hbm, sizes, sems.at[0]),
        pltpu.make_async_copy(pattern_hbm, pattern, sems.at[1]),
        pltpu.make_async_copy(density_hbm, density, sems.at[2]),
    ]
    for copy in copies:
        copy.start()
    col_blocks, row_blocks = pattern.shape
    first_row = (lax.axis_index("xh") * NY + lax.axis_index("y")) * row_blocks
    first_col = ((lax.axis_index("xl") * NZ + lax.axis_index("z")) * 2 + lax.axis_index("c")) * col_blocks
    sub = lax.broadcasted_iota(jnp.int32, (BS, 2 * BS), 0)
    lane = lax.broadcasted_iota(jnp.int32, (BS, 2 * BS), 1)
    left = lane < BS
    for copy in copies:
        copy.wait()
    size_col = jnp.where(left, sizes[first_col], sizes[first_col + 1])
    valid_col = (jnp.where(left, lane, lane - BS) < size_col).astype(F32)
    for i in range(row_blocks):
        stored = jnp.where(left, pattern[0, i], pattern[1, i]).astype(F32)
        valid = (sub < sizes[first_row + i]).astype(F32) * valid_col * stored
        out[i * BS : (i + 1) * BS, :] = density[i * BS : (i + 1) * BS, :] * valid


def split(x):
    hi = x.astype(BF16)
    return hi, (x - hi.astype(F32)).astype(BF16)


dot = functools.partial(jnp.dot, preferred_element_type=F32)


def split_dot(a, bh, bl):
    ah, al = split(a)
    return dot(ah, bh) + (dot(ah, bl) + dot(al, bh))


def put_halves(total, mine, other):
    same = lax.axis_index("xl") == lax.axis_index("xh")
    near, far = total[:, :128], total[:, 128:]
    mine[...] = jnp.where(same, near, far)
    other[...] = jnp.where(same, far, near)


def pack_kernel(offsets, *refs):
    n = len(offsets)
    near, far = refs[:n], refs[n : 2 * n]
    hi, lo, give = refs[2 * n :]
    y = lax.axis_index("y")
    c = lax.axis_index("c")
    for k, off in enumerate(offsets):
        first = 3 * lax.rem(y + (off + NY), NY)
        for t in range(3):
            rows = slice(t * 128, (t + 1) * 128)
            unit = jnp.concatenate([near[k][rows, :], far[k][rows, :]], axis=1)
            hi[first + t], lo[first + t] = split(unit)

            @pl.when(lax.rem(first + t, 2) != c)
            def _():
                give[(first + t) // 2] = unit


def pack(offsets, near, far):
    rows, cols = near[0].shape
    args = near + far
    half = jax.ShapeDtypeStruct((2 * NZ, 128, 2 * cols), BF16)
    return pl.pallas_call(
        functools.partial(pack_kernel, tuple(offsets)),
        out_shape=(half, half, jax.ShapeDtypeStruct((NZ, 128, 2 * cols), F32)),
        in_specs=[VM] * len(args),
        out_specs=(VM,) * 3,
        compiler_params=PARAMS,
    )(*args)


def rows_kernel(hi, lo, took, rows_hi, rows_lo):
    c = lax.axis_index("c")
    for z in range(NZ):
        rows_hi[z, :, :256] = hi[2 * z + c]
        rows_lo[z, :, :256] = lo[2 * z + c]
        rows_hi[z, :, 256:], rows_lo[z, :, 256:] = split(took[z])


def phase_rows(hi, lo, took):
    units, depth, cols = took.shape
    half = jax.ShapeDtypeStruct((units, depth, 2 * cols), BF16)
    return pl.pallas_call(
        rows_kernel,
        out_shape=(half, half),
        in_specs=[VM] * 3,
        out_specs=(VM, VM),
        compiler_params=PARAMS,
    )(hi, lo, took)


def first_kernel(left, hi, lo, mine, other, held, sems):
    parts, per = held.shape[:2]
    copies = [
        pltpu.make_async_copy(left.at[pl.ds(per * p, per)], held.at[p], sems.at[p]) for p in range(parts)
    ]
    for copy in copies:
        copy.start()
    for copy in copies:
        copy.wait()
    acc = None
    for z in range(NZ):
        u = 2 * z
        p, k = divmod(u, per)
        a = jnp.concatenate([held[p, k], held[p, k + 1]], axis=1)
        bh = jnp.concatenate([hi[u], hi[u + 1]], axis=0)
        bl = jnp.concatenate([lo[u], lo[u + 1]], axis=0)
        term = split_dot(a, bh, bl)
        acc = term if acc is None else acc + term
    put_halves(acc, mine, other)


def first_product(left, hi, lo):
    units, rows, cols = left.shape
    parts = 6
    block = jax.ShapeDtypeStruct((rows, cols), F32)
    return pl.pallas_call(
        first_kernel,
        out_shape=(block, block),
        in_specs=[HB, VM, VM],
        out_specs=(VM, VM),
        scratch_shapes=[
            pltpu.VMEM((parts, units // parts, rows, cols), F32),
            pltpu.SemaphoreType.DMA((parts,)),
        ],
        compiler_params=WIDE,
        cost_estimate=pl.CostEstimate(
            flops=NZ * 3 * 2 * rows * 2 * cols * 2 * cols, bytes_accessed=0, transcendentals=0
        ),
    )(left, hi, lo)


def second_kernel(offsets, has_acc, last, hi, lo, *refs):
    n = len(offsets)
    acc = refs[n][...] if has_acc else None
    outs = refs[n + has_acc :]
    z = lax.axis_index("z")
    at = [lax.rem(z + (off + NZ), NZ) for off in offsets]
    for k in range(0, n, 2):
        a = jnp.concatenate([refs[k][...], refs[k + 1][...]], axis=1)
        bh = jnp.concatenate([hi[at[k]], hi[at[k + 1]]], axis=0)
        bl = jnp.concatenate([lo[at[k]], lo[at[k + 1]]], axis=0)
        term = split_dot(a, bh, bl)
        acc = term if acc is None else acc + term
    if last:
        outs[0][...] = acc[:, :256]
        outs[1][...] = acc[:, 256:]
    else:
        outs[0][...] = acc


def second_product(operand, blocks, acc=None, last=False):
    offsets = tuple(off for off, _ in blocks)
    rows, cols = blocks[0][1].shape
    args = list(operand) + [x for _, x in blocks] + ([] if acc is None else [acc])
    if last:
        shapes = (jax.ShapeDtypeStruct((rows, 2 * cols), F32),) * 2
    else:
        shapes = jax.ShapeDtypeStruct((rows, 4 * cols), F32)
    return pl.pallas_call(
        functools.partial(second_kernel, offsets, acc is not None, last),
        out_shape=shapes,
        in_specs=[VM] * len(args),
        out_specs=(VM, VM) if last else VM,
        compiler_params=PARAMS,
        cost_estimate=pl.CostEstimate(
            flops=len(offsets) * 3 * 2 * rows * cols * 4 * cols, bytes_accessed=0, transcendentals=0
        ),
    )(*args)


def join_kernel(own, both, mine, other):
    put_halves(own[...] + both[1 - lax.axis_index("c")], mine, other)


def join(own, give):
    both = lax.all_gather(give, "c", axis=0)
    rows, cols = own.shape
    block = jax.ShapeDtypeStruct((rows, cols // 2), F32)
    return pl.pallas_call(
        join_kernel,
        out_shape=(block, block),
        in_specs=[VM, VM],
        out_specs=(VM, VM),
        compiler_params=PARAMS,
    )(own, both)


def filter_kernel(final, kept, mine, pair, *refs):
    other = 1 - lax.axis_index("xl")
    lane = lax.broadcasted_iota(jnp.int32, (BS, 2 * BS), 1)
    for i in range(kept.shape[1]):
        strip = slice(i * BS, (i + 1) * BS)
        filt = jnp.where(lane < BS, kept[0, i], kept[1, i]).astype(F32)
        total = filt * (mine[strip, :] + pair[other, strip, :])
        if final:
            square = refs[0][strip, :]
            refs[1][strip, :] = square
            refs[2][strip, :] = 3.0 * square - 2.0 * total
        else:
            refs[0][strip, :] = total


def filtered(kept, halves, square=None):
    mine, other = halves
    final = square is not None
    pair = lax.all_gather(other, "xl", axis=0)
    args = [kept, mine, pair] + ([square] if final else [])
    block = jax.ShapeDtypeStruct(mine.shape, F32)
    return pl.pallas_call(
        functools.partial(filter_kernel, final),
        out_shape=(block, block) if final else block,
        in_specs=[SM] + [VM] * (len(args) - 1),
        out_specs=(VM, VM) if final else VM,
        compiler_params=PARAMS,
    )(*args)


def shift(x, axis, step):
    n = SIZES[AXES.index(axis)]
    return lax.ppermute(x, axis, [(i, (i + step) % n) for i in range(n)])


def together(*xs):
    return lax.optimization_barrier(xs)


def chain(x, axis, step, count):
    out = []
    for _ in range(count):
        x = shift(x, axis, step)
        out.append(x)
    return out


def body(density, atom_sizes, pattern, kept):
    pattern = pattern.T
    masked = pl.pallas_call(
        mask_kernel,
        out_shape=jax.ShapeDtypeStruct(density.shape, F32),
        in_specs=[HB] * 3,
        out_specs=VM,
        scratch_shapes=[
            pltpu.SMEM(atom_sizes.shape, jnp.int32),
            pltpu.SMEM(pattern.shape, jnp.int32),
            pltpu.VMEM(density.shape, F32),
            pltpu.SemaphoreType.DMA((3,)),
        ],
        compiler_params=WHOLE,
    )(atom_sizes, pattern, density)

    left = lax.all_gather(masked, ("z", "c"), axis=0)

    near = lax.ppermute(masked, ("xh", "xl"), [(0, 0), (1, 2), (2, 1), (3, 3)])
    far = lax.ppermute(masked, ("xh", "xl"), [(1, 0), (2, 3), (0, 2), (3, 1)])
    near_up, near_down = chain(near, "y", 1, 4), chain(near, "y", -1, 3)
    far_up, far_down = chain(far, "y", 1, 3), chain(far, "y", -1, 4)
    offsets = [0, -1, 1, -2, 2, -3, 3, 4]
    near = [near] + [x for pair in zip(near_up, near_down) for x in pair] + [near_up[3]]
    far = [far] + [x for pair in zip(far_up, far_down) for x in pair] + [far_down[3]]
    hi, lo, give = pack(offsets, near, far)
    took = shift(give, "c", 1)
    mine, other, took = together(*first_product(left, hi, lo), took)
    square = filtered(kept.T, (mine, other))

    operand = phase_rows(hi, lo, took)
    away = shift(square, "z", 6)
    up, down = chain(square, "z", 1, 2), chain(square, "z", -1, 2)
    down[1], away = together(down[1], away)
    up += chain(up[1], "z", 1, 2)
    down += chain(down[1], "z", -1, 2)
    blocks = [(0, square)]
    for s in range(3):
        blocks += [(-s - 1, up[s]), (s + 1, down[s])]
    blocks += [(6, away), (-4, up[3]), (4, down[3]), (5, shift(away, "z", 1)), (-5, shift(away, "z", -1))]
    acc = second_product(operand, blocks[:4])
    acc = second_product(operand, blocks[4:8], acc)
    halves = join(*second_product(operand, blocks[8:], acc, last=True))
    return filtered(kept.T, halves, square)


def solution(mesh):
    fine = Mesh(mesh.devices.reshape(SIZES), AXES)
    placed = (P(ROW, COL), P(), P(ROW, COL), P(ROW, COL))
    return jax.shard_map(
        body,
        mesh=fine,
        in_specs=placed,
        out_specs=(P(ROW, COL), P(ROW, COL)),
        check_vma=False,
    )
```

```python
import functools

import jax
import jax.numpy as jnp
from jax import lax
from jax.experimental import pallas as pl
from jax.experimental.pallas import tpu as pltpu
from jax.sharding import Mesh, PartitionSpec as P

BS = 64
AXES = ("xh", "y", "xl", "z", "c")
SIZES = (2, 8, 2, 12, 2)
NY = 8
NZ = 12
ROW = ("xh", "y")
COL = ("xl", "z", "c")
F32 = jnp.float32
BF16 = jnp.bfloat16
VM = pl.BlockSpec(memory_space=pltpu.VMEM)
SM = pl.BlockSpec(memory_space=pltpu.SMEM)
HB = pl.BlockSpec(memory_space=pltpu.HBM)
PARAMS = pltpu.CompilerParams(vmem_limit_bytes=32 * 1024 * 1024)
WIDE = pltpu.CompilerParams(vmem_limit_bytes=50 * 1024 * 1024)
WHOLE = pltpu.CompilerParams(vmem_limit_bytes=64 * 1024 * 1024 - 128 * 1024)


def mask_kernel(sizes_hbm, pattern_hbm, density_hbm, out, sizes, pattern, density, sems):
    copies = [
        pltpu.make_async_copy(sizes_hbm, sizes, sems.at[0]),
        pltpu.make_async_copy(pattern_hbm, pattern, sems.at[1]),
        pltpu.make_async_copy(density_hbm, density, sems.at[2]),
    ]
    for copy in copies:
        copy.start()
    col_blocks, row_blocks = pattern.shape
    first_row = (lax.axis_index("xh") * NY + lax.axis_index("y")) * row_blocks
    first_col = ((lax.axis_index("xl") * NZ + lax.axis_index("z")) * 2 + lax.axis_index("c")) * col_blocks
    sub = lax.broadcasted_iota(jnp.int32, (BS, 2 * BS), 0)
    lane = lax.broadcasted_iota(jnp.int32, (BS, 2 * BS), 1)
    left = lane < BS
    for copy in copies:
        copy.wait()
    size_col = jnp.where(left, sizes[first_col], sizes[first_col + 1])
    valid_col = (jnp.where(left, lane, lane - BS) < size_col).astype(F32)
    for i in range(row_blocks):
        stored = jnp.where(left, pattern[0, i], pattern[1, i]).astype(F32)
        valid = (sub < sizes[first_row + i]).astype(F32) * valid_col * stored
        out[i * BS : (i + 1) * BS, :] = density[i * BS : (i + 1) * BS, :] * valid


def split(x):
    hi = x.astype(BF16)
    return hi, (x - hi.astype(F32)).astype(BF16)


dot = functools.partial(jnp.dot, preferred_element_type=F32)


def split_dot(a, bh, bl):
    ah, al = split(a)
    return dot(ah, bh) + (dot(ah, bl) + dot(al, bh))


def put_halves(total, mine, other):
    same = lax.axis_index("xl") == lax.axis_index("xh")
    near, far = total[:, :128], total[:, 128:]
    mine[...] = jnp.where(same, near, far)
    other[...] = jnp.where(same, far, near)


def pack_kernel(offsets, *refs):
    n = len(offsets)
    near, far = refs[:n], refs[n : 2 * n]
    hi, lo, give = refs[2 * n :]
    y = lax.axis_index("y")
    c = lax.axis_index("c")
    for k, off in enumerate(offsets):
        first = 3 * lax.rem(y + (off + NY), NY)
        for t in range(3):
            rows = slice(t * 128, (t + 1) * 128)
            unit = jnp.concatenate([near[k][rows, :], far[k][rows, :]], axis=1)
            hi[first + t], lo[first + t] = split(unit)

            @pl.when(lax.rem(first + t, 2) != c)
            def _():
                give[(first + t) // 2] = unit


def pack(offsets, near, far):
    rows, cols = near[0].shape
    args = near + far
    half = jax.ShapeDtypeStruct((2 * NZ, 128, 2 * cols), BF16)
    return pl.pallas_call(
        functools.partial(pack_kernel, tuple(offsets)),
        out_shape=(half, half, jax.ShapeDtypeStruct((NZ, 128, 2 * cols), F32)),
        in_specs=[VM] * len(args),
        out_specs=(VM,) * 3,
        compiler_params=PARAMS,
    )(*args)


def rows_kernel(hi, lo, took, rows_hi, rows_lo):
    c = lax.axis_index("c")
    for z in range(NZ):
        rows_hi[z, :, :256] = hi[2 * z + c]
        rows_lo[z, :, :256] = lo[2 * z + c]
        rows_hi[z, :, 256:], rows_lo[z, :, 256:] = split(took[z])


def phase_rows(hi, lo, took):
    units, depth, cols = took.shape
    half = jax.ShapeDtypeStruct((units, depth, 2 * cols), BF16)
    return pl.pallas_call(
        rows_kernel,
        out_shape=(half, half),
        in_specs=[VM] * 3,
        out_specs=(VM, VM),
        compiler_params=PARAMS,
    )(hi, lo, took)


def first_kernel(left, hi, lo, mine, other, held, sems):
    parts, per = held.shape[:2]
    copies = [
        pltpu.make_async_copy(left.at[pl.ds(per * p, per)], held.at[p], sems.at[p]) for p in range(parts)
    ]
    half = parts // 2
    for copy in copies[:half]:
        copy.start()
    acc = None
    for z in range(NZ):
        if z == 0:
            for first, second in zip(copies[:half], copies[half:]):
                first.wait()
                second.start()
        if z == NZ // 2:
            for copy in copies[half:]:
                copy.wait()
        u = 2 * z
        p, k = divmod(u, per)
        a = jnp.concatenate([held[p, k], held[p, k + 1]], axis=1)
        bh = jnp.concatenate([hi[u], hi[u + 1]], axis=0)
        bl = jnp.concatenate([lo[u], lo[u + 1]], axis=0)
        term = split_dot(a, bh, bl)
        acc = term if acc is None else acc + term
    put_halves(acc, mine, other)


def first_product(left, hi, lo):
    units, rows, cols = left.shape
    parts = 6
    block = jax.ShapeDtypeStruct((rows, cols), F32)
    return pl.pallas_call(
        first_kernel,
        out_shape=(block, block),
        in_specs=[HB, VM, VM],
        out_specs=(VM, VM),
        scratch_shapes=[
            pltpu.VMEM((parts, units // parts, rows, cols), F32),
            pltpu.SemaphoreType.DMA((parts,)),
        ],
        compiler_params=WIDE,
        cost_estimate=pl.CostEstimate(
            flops=NZ * 3 * 2 * rows * 2 * cols * 2 * cols, bytes_accessed=0, transcendentals=0
        ),
    )(left, hi, lo)


def second_kernel(offsets, has_acc, last, hi, lo, *refs):
    n = len(offsets)
    acc = refs[n][...] if has_acc else None
    outs = refs[n + has_acc :]
    z = lax.axis_index("z")
    at = [lax.rem(z + (off + NZ), NZ) for off in offsets]
    for k in range(0, n, 2):
        pair = range(k, min(k + 2, n))
        a = jnp.concatenate([refs[i][...] for i in pair], axis=1)
        bh = jnp.concatenate([hi[at[i]] for i in pair], axis=0)
        bl = jnp.concatenate([lo[at[i]] for i in pair], axis=0)
        term = split_dot(a, bh, bl)
        acc = term if acc is None else acc + term
    if last:
        outs[0][...] = acc[:, :256]
        outs[1][...] = acc[:, 256:]
    else:
        outs[0][...] = acc


def second_product(operand, blocks, acc=None, last=False):
    offsets = tuple(off for off, _ in blocks)
    rows, cols = blocks[0][1].shape
    args = list(operand) + [x for _, x in blocks] + ([] if acc is None else [acc])
    if last:
        shapes = (jax.ShapeDtypeStruct((rows, 2 * cols), F32),) * 2
    else:
        shapes = jax.ShapeDtypeStruct((rows, 4 * cols), F32)
    return pl.pallas_call(
        functools.partial(second_kernel, offsets, acc is not None, last),
        out_shape=shapes,
        in_specs=[VM] * len(args),
        out_specs=(VM, VM) if last else VM,
        compiler_params=PARAMS,
        cost_estimate=pl.CostEstimate(
            flops=len(offsets) * 3 * 2 * rows * cols * 4 * cols, bytes_accessed=0, transcendentals=0
        ),
    )(*args)


def join_kernel(own, both, mine, other):
    put_halves(own[...] + both[1 - lax.axis_index("c")], mine, other)


def join(own, give):
    both = lax.all_gather(give, "c", axis=0)
    rows, cols = own.shape
    block = jax.ShapeDtypeStruct((rows, cols // 2), F32)
    return pl.pallas_call(
        join_kernel,
        out_shape=(block, block),
        in_specs=[VM, VM],
        out_specs=(VM, VM),
        compiler_params=PARAMS,
    )(own, both)


def filter_kernel(final, kept, mine, pair, *refs):
    other = 1 - lax.axis_index("xl")
    lane = lax.broadcasted_iota(jnp.int32, (BS, 2 * BS), 1)
    for i in range(kept.shape[1]):
        strip = slice(i * BS, (i + 1) * BS)
        filt = jnp.where(lane < BS, kept[0, i], kept[1, i]).astype(F32)
        total = filt * (mine[strip, :] + pair[other, strip, :])
        if final:
            square = refs[0][strip, :]
            refs[1][strip, :] = square
            refs[2][strip, :] = 3.0 * square - 2.0 * total
        else:
            refs[0][strip, :] = total


def filtered(kept, halves, square=None):
    mine, other = halves
    final = square is not None
    pair = lax.all_gather(other, "xl", axis=0)
    args = [kept, mine, pair] + ([square] if final else [])
    block = jax.ShapeDtypeStruct(mine.shape, F32)
    return pl.pallas_call(
        functools.partial(filter_kernel, final),
        out_shape=(block, block) if final else block,
        in_specs=[SM] + [VM] * (len(args) - 1),
        out_specs=(VM, VM) if final else VM,
        compiler_params=PARAMS,
    )(*args)


def shift(x, axis, step):
    n = SIZES[AXES.index(axis)]
    return lax.ppermute(x, axis, [(i, (i + step) % n) for i in range(n)])


def together(*xs):
    return lax.optimization_barrier(xs)


def chain(x, axis, step, count):
    out = []
    for _ in range(count):
        x = shift(x, axis, step)
        out.append(x)
    return out


def body(density, atom_sizes, pattern, kept):
    pattern = pattern.T
    masked = pl.pallas_call(
        mask_kernel,
        out_shape=jax.ShapeDtypeStruct(density.shape, F32),
        in_specs=[HB] * 3,
        out_specs=VM,
        scratch_shapes=[
            pltpu.SMEM(atom_sizes.shape, jnp.int32),
            pltpu.SMEM(pattern.shape, jnp.int32),
            pltpu.VMEM(density.shape, F32),
            pltpu.SemaphoreType.DMA((3,)),
        ],
        compiler_params=WHOLE,
    )(atom_sizes, pattern, density)

    left = lax.all_gather(masked, ("z", "c"), axis=0)

    near = lax.ppermute(masked, ("xh", "xl"), [(0, 0), (1, 2), (2, 1), (3, 3)])
    far = lax.ppermute(masked, ("xh", "xl"), [(1, 0), (2, 3), (0, 2), (3, 1)])
    near_up, near_down = chain(near, "y", 1, 4), chain(near, "y", -1, 3)
    far_up, far_down = chain(far, "y", 1, 3), chain(far, "y", -1, 4)
    offsets = [0, -1, 1, -2, 2, -3, 3, 4]
    near = [near] + [x for pair in zip(near_up, near_down) for x in pair] + [near_up[3]]
    far = [far] + [x for pair in zip(far_up, far_down) for x in pair] + [far_down[3]]
    hi, lo, give = pack(offsets, near, far)
    took = shift(give, "c", 1)
    mine, other, took = together(*first_product(left, hi, lo), took)
    square = filtered(kept.T, (mine, other))

    operand = phase_rows(hi, lo, took)
    up, down = chain(square, "z", 1, 6), chain(square, "z", -1, 5)
    blocks = [(0, square)]
    for s in range(5):
        blocks += [(-s - 1, up[s]), (s + 1, down[s])]
    blocks.append((-6, up[5]))
    acc = second_product(operand, blocks[:4])
    acc = second_product(operand, blocks[4:8], acc)
    acc = second_product(operand, blocks[8:11], acc)
    halves = join(*second_product(operand, blocks[11:], acc, last=True))
    return filtered(kept.T, halves, square)


def solution(mesh):
    fine = Mesh(mesh.devices.reshape(SIZES), AXES)
    placed = (P(ROW, COL), P(), P(ROW, COL), P(ROW, COL))
    return jax.shard_map(
        body,
        mesh=fine,
        in_specs=placed,
        out_specs=(P(ROW, COL), P(ROW, COL)),
        check_vma=False,
    )
```

```python
import functools

import jax
import jax.numpy as jnp
from jax import lax
from jax.experimental import pallas as pl
from jax.experimental.pallas import tpu as pltpu
from jax.sharding import Mesh, PartitionSpec as P

BS = 64
AXES = ("xh", "y", "xl", "z", "c")
SIZES = (2, 8, 2, 12, 2)
NY = 8
NZ = 12
ROW = ("xh", "y")
COL = ("xl", "z", "c")
F32 = jnp.float32
BF16 = jnp.bfloat16
VM = pl.BlockSpec(memory_space=pltpu.VMEM)
SM = pl.BlockSpec(memory_space=pltpu.SMEM)
HB = pl.BlockSpec(memory_space=pltpu.HBM)
PARAMS = pltpu.CompilerParams(vmem_limit_bytes=32 * 1024 * 1024)
WIDE = pltpu.CompilerParams(vmem_limit_bytes=50 * 1024 * 1024)
WHOLE = pltpu.CompilerParams(vmem_limit_bytes=64 * 1024 * 1024 - 128 * 1024)


def mask_kernel(sizes_hbm, pattern_hbm, density_hbm, out, sizes, pattern, density, sems):
    copies = [
        pltpu.make_async_copy(sizes_hbm, sizes, sems.at[0]),
        pltpu.make_async_copy(pattern_hbm, pattern, sems.at[1]),
        pltpu.make_async_copy(density_hbm, density, sems.at[2]),
    ]
    for copy in copies:
        copy.start()
    col_blocks, row_blocks = pattern.shape
    first_row = (lax.axis_index("xh") * NY + lax.axis_index("y")) * row_blocks
    first_col = ((lax.axis_index("xl") * NZ + lax.axis_index("z")) * 2 + lax.axis_index("c")) * col_blocks
    sub = lax.broadcasted_iota(jnp.int32, (BS, 2 * BS), 0)
    lane = lax.broadcasted_iota(jnp.int32, (BS, 2 * BS), 1)
    left = lane < BS
    for copy in copies:
        copy.wait()
    size_col = jnp.where(left, sizes[first_col], sizes[first_col + 1])
    valid_col = (jnp.where(left, lane, lane - BS) < size_col).astype(F32)
    for i in range(row_blocks):
        stored = jnp.where(left, pattern[0, i], pattern[1, i]).astype(F32)
        valid = (sub < sizes[first_row + i]).astype(F32) * valid_col * stored
        out[i * BS : (i + 1) * BS, :] = density[i * BS : (i + 1) * BS, :] * valid


def split(x):
    hi = x.astype(BF16)
    return hi, (x - hi.astype(F32)).astype(BF16)


dot = functools.partial(jnp.dot, preferred_element_type=F32)


def split_dot(a, bh, bl):
    ah, al = split(a)
    return dot(ah, bh) + (dot(ah, bl) + dot(al, bh))


def put_halves(total, mine, other):
    same = lax.axis_index("xl") == lax.axis_index("xh")
    near, far = total[:, :128], total[:, 128:]
    mine[...] = jnp.where(same, near, far)
    other[...] = jnp.where(same, far, near)


def pack_kernel(offsets, *refs):
    n = len(offsets)
    near, far = refs[:n], refs[n : 2 * n]
    hi, lo, give = refs[2 * n :]
    y = lax.axis_index("y")
    c = lax.axis_index("c")
    for k, off in enumerate(offsets):
        first = 3 * lax.rem(y + (off + NY), NY)
        for t in range(3):
            rows = slice(t * 128, (t + 1) * 128)
            unit = jnp.concatenate([near[k][rows, :], far[k][rows, :]], axis=1)
            hi[first + t], lo[first + t] = split(unit)

            @pl.when(lax.rem(first + t, 2) != c)
            def _():
                give[(first + t) // 2] = unit


def pack(offsets, near, far):
    rows, cols = near[0].shape
    args = near + far
    half = jax.ShapeDtypeStruct((2 * NZ, 128, 2 * cols), BF16)
    return pl.pallas_call(
        functools.partial(pack_kernel, tuple(offsets)),
        out_shape=(half, half, jax.ShapeDtypeStruct((NZ, 128, 2 * cols), F32)),
        in_specs=[VM] * len(args),
        out_specs=(VM,) * 3,
        compiler_params=PARAMS,
    )(*args)


def rows_kernel(hi, lo, took, rows_hi, rows_lo):
    c = lax.axis_index("c")
    for z in range(NZ):
        rows_hi[z, :, :256] = hi[2 * z + c]
        rows_lo[z, :, :256] = lo[2 * z + c]
        rows_hi[z, :, 256:], rows_lo[z, :, 256:] = split(took[z])


def phase_rows(hi, lo, took):
    units, depth, cols = took.shape
    half = jax.ShapeDtypeStruct((units, depth, 2 * cols), BF16)
    return pl.pallas_call(
        rows_kernel,
        out_shape=(half, half),
        in_specs=[VM] * 3,
        out_specs=(VM, VM),
        compiler_params=PARAMS,
    )(hi, lo, took)


def first_kernel(left, hi, lo, mine, other, held, sems):
    parts, per = held.shape[:2]
    copies = [
        pltpu.make_async_copy(left.at[pl.ds(per * p, per)], held.at[p], sems.at[p]) for p in range(parts)
    ]
    for copy in copies:
        copy.start()
    for copy in copies:
        copy.wait()
    acc = None
    for z in range(NZ):
        u = 2 * z
        p, k = divmod(u, per)
        a = jnp.concatenate([held[p, k], held[p, k + 1]], axis=1)
        bh = jnp.concatenate([hi[u], hi[u + 1]], axis=0)
        bl = jnp.concatenate([lo[u], lo[u + 1]], axis=0)
        term = split_dot(a, bh, bl)
        acc = term if acc is None else acc + term
    put_halves(acc, mine, other)


def first_product(left, hi, lo):
    units, rows, cols = left.shape
    parts = 6
    block = jax.ShapeDtypeStruct((rows, cols), F32)
    return pl.pallas_call(
        first_kernel,
        out_shape=(block, block),
        in_specs=[HB, VM, VM],
        out_specs=(VM, VM),
        scratch_shapes=[
            pltpu.VMEM((parts, units // parts, rows, cols), F32),
            pltpu.SemaphoreType.DMA((parts,)),
        ],
        compiler_params=WIDE,
        cost_estimate=pl.CostEstimate(
            flops=NZ * 3 * 2 * rows * 2 * cols * 2 * cols, bytes_accessed=0, transcendentals=0
        ),
    )(left, hi, lo)


def second_kernel(offsets, has_acc, last, hi, lo, *refs):
    n = len(offsets)
    acc = refs[n][...] if has_acc else None
    outs = refs[n + has_acc :]
    z = lax.axis_index("z")
    at = [lax.rem(z + (off + NZ), NZ) for off in offsets]
    for k in range(0, n, 2):
        pair = range(k, min(k + 2, n))
        a = jnp.concatenate([refs[i][...] for i in pair], axis=1)
        bh = jnp.concatenate([hi[at[i]] for i in pair], axis=0)
        bl = jnp.concatenate([lo[at[i]] for i in pair], axis=0)
        term = split_dot(a, bh, bl)
        acc = term if acc is None else acc + term
    if last:
        outs[0][...] = acc[:, :256]
        outs[1][...] = acc[:, 256:]
    else:
        outs[0][...] = acc


def second_product(operand, blocks, acc=None, last=False):
    offsets = tuple(off for off, _ in blocks)
    rows, cols = blocks[0][1].shape
    args = list(operand) + [x for _, x in blocks] + ([] if acc is None else [acc])
    if last:
        shapes = (jax.ShapeDtypeStruct((rows, 2 * cols), F32),) * 2
    else:
        shapes = jax.ShapeDtypeStruct((rows, 4 * cols), F32)
    return pl.pallas_call(
        functools.partial(second_kernel, offsets, acc is not None, last),
        out_shape=shapes,
        in_specs=[VM] * len(args),
        out_specs=(VM, VM) if last else VM,
        compiler_params=PARAMS,
        cost_estimate=pl.CostEstimate(
            flops=len(offsets) * 3 * 2 * rows * cols * 4 * cols, bytes_accessed=0, transcendentals=0
        ),
    )(*args)


def join_kernel(own, both, mine, other):
    put_halves(own[...] + both[1 - lax.axis_index("c")], mine, other)


def join(own, give):
    both = lax.all_gather(give, "c", axis=0)
    rows, cols = own.shape
    block = jax.ShapeDtypeStruct((rows, cols // 2), F32)
    return pl.pallas_call(
        join_kernel,
        out_shape=(block, block),
        in_specs=[VM, VM],
        out_specs=(VM, VM),
        compiler_params=PARAMS,
    )(own, both)


def filter_kernel(final, kept, mine, pair, *refs):
    other = 1 - lax.axis_index("xl")
    lane = lax.broadcasted_iota(jnp.int32, (BS, 2 * BS), 1)
    for i in range(kept.shape[1]):
        strip = slice(i * BS, (i + 1) * BS)
        filt = jnp.where(lane < BS, kept[0, i], kept[1, i]).astype(F32)
        total = filt * (mine[strip, :] + pair[other, strip, :])
        if final:
            square = refs[0][strip, :]
            refs[1][strip, :] = square
            refs[2][strip, :] = 3.0 * square - 2.0 * total
        else:
            refs[0][strip, :] = total


def filtered(kept, halves, square=None):
    mine, other = halves
    final = square is not None
    pair = lax.all_gather(other, "xl", axis=0)
    args = [kept, mine, pair] + ([square] if final else [])
    block = jax.ShapeDtypeStruct(mine.shape, F32)
    return pl.pallas_call(
        functools.partial(filter_kernel, final),
        out_shape=(block, block) if final else block,
        in_specs=[SM] + [VM] * (len(args) - 1),
        out_specs=(VM, VM) if final else VM,
        compiler_params=PARAMS,
    )(*args)


def shift(x, axis, step):
    n = SIZES[AXES.index(axis)]
    return lax.ppermute(x, axis, [(i, (i + step) % n) for i in range(n)])


def together(*xs):
    return lax.optimization_barrier(xs)


def chain(x, axis, step, count):
    out = []
    for _ in range(count):
        x = shift(x, axis, step)
        out.append(x)
    return out


def body(density, atom_sizes, pattern, kept):
    pattern = pattern.T
    masked = pl.pallas_call(
        mask_kernel,
        out_shape=jax.ShapeDtypeStruct(density.shape, F32),
        in_specs=[HB] * 3,
        out_specs=VM,
        scratch_shapes=[
            pltpu.SMEM(atom_sizes.shape, jnp.int32),
            pltpu.SMEM(pattern.shape, jnp.int32),
            pltpu.VMEM(density.shape, F32),
            pltpu.SemaphoreType.DMA((3,)),
        ],
        compiler_params=WHOLE,
    )(atom_sizes, pattern, density)

    left = lax.all_gather(masked, ("z", "c"), axis=0)

    near = lax.ppermute(masked, ("xh", "xl"), [(0, 0), (1, 2), (2, 1), (3, 3)])
    far = lax.ppermute(masked, ("xh", "xl"), [(1, 0), (2, 3), (0, 2), (3, 1)])
    near_up, near_down = chain(near, "y", 1, 4), chain(near, "y", -1, 3)
    far_up, far_down = chain(far, "y", 1, 3), chain(far, "y", -1, 4)
    offsets = [0, -1, 1, -2, 2, -3, 3, 4]
    near = [near] + [x for pair in zip(near_up, near_down) for x in pair] + [near_up[3]]
    far = [far] + [x for pair in zip(far_up, far_down) for x in pair] + [far_down[3]]
    hi, lo, give = pack(offsets, near, far)
    took = shift(give, "c", 1)
    mine, other, took = together(*first_product(left, hi, lo), took)
    square = filtered(kept.T, (mine, other))

    operand = phase_rows(hi, lo, took)
    up, down = chain(square, "z", 1, 6), chain(square, "z", -1, 5)
    blocks = [(0, square)]
    for s in range(5):
        blocks += [(-s - 1, up[s]), (s + 1, down[s])]
    blocks.append((-6, up[5]))
    acc = second_product(operand, blocks[:4])
    acc = second_product(operand, blocks[4:8], acc)
    acc = second_product(operand, blocks[8:11], acc)
    halves = join(*second_product(operand, blocks[11:], acc, last=True))
    return filtered(kept.T, halves, square)


def solution(mesh):
    fine = Mesh(mesh.devices.reshape(SIZES), AXES)
    placed = (P(ROW, COL), P(), P(ROW, COL), P(ROW, COL))
    return jax.shard_map(
        body,
        mesh=fine,
        in_specs=placed,
        out_specs=(P(ROW, COL), P(ROW, COL)),
        check_vma=False,
    )
```

```python
import functools

import jax
import jax.numpy as jnp
from jax import lax
from jax.experimental import pallas as pl
from jax.experimental.pallas import tpu as pltpu
from jax.sharding import Mesh, PartitionSpec as P

BS = 64
AXES = ("xh", "y", "xl", "z", "c")
SIZES = (2, 8, 2, 12, 2)
NY = 8
NZ = 12
ROW = ("xh", "y")
COL = ("xl", "z", "c")
F32 = jnp.float32
BF16 = jnp.bfloat16
VM = pl.BlockSpec(memory_space=pltpu.VMEM)
SM = pl.BlockSpec(memory_space=pltpu.SMEM)
HB = pl.BlockSpec(memory_space=pltpu.HBM)
PARAMS = pltpu.CompilerParams(vmem_limit_bytes=32 * 1024 * 1024)
WIDE = pltpu.CompilerParams(vmem_limit_bytes=50 * 1024 * 1024)
WHOLE = pltpu.CompilerParams(vmem_limit_bytes=64 * 1024 * 1024 - 128 * 1024)


def mask_kernel(sizes_hbm, pattern_hbm, density_hbm, out, sizes, pattern, density, sems):
    copies = [
        pltpu.make_async_copy(sizes_hbm, sizes, sems.at[0]),
        pltpu.make_async_copy(pattern_hbm, pattern, sems.at[1]),
        pltpu.make_async_copy(density_hbm, density, sems.at[2]),
    ]
    for copy in copies:
        copy.start()
    col_blocks, row_blocks = pattern.shape
    first_row = (lax.axis_index("xh") * NY + lax.axis_index("y")) * row_blocks
    first_col = ((lax.axis_index("xl") * NZ + lax.axis_index("z")) * 2 + lax.axis_index("c")) * col_blocks
    sub = lax.broadcasted_iota(jnp.int32, (BS, 2 * BS), 0)
    lane = lax.broadcasted_iota(jnp.int32, (BS, 2 * BS), 1)
    left = lane < BS
    for copy in copies:
        copy.wait()
    size_col = jnp.where(left, sizes[first_col], sizes[first_col + 1])
    valid_col = (jnp.where(left, lane, lane - BS) < size_col).astype(F32)
    for i in range(row_blocks):
        stored = jnp.where(left, pattern[0, i], pattern[1, i]).astype(F32)
        valid = (sub < sizes[first_row + i]).astype(F32) * valid_col * stored
        out[i * BS : (i + 1) * BS, :] = density[i * BS : (i + 1) * BS, :] * valid


def split(x):
    hi = x.astype(BF16)
    return hi, (x - hi.astype(F32)).astype(BF16)


dot = functools.partial(jnp.dot, preferred_element_type=F32)


def split_dot(a, bh, bl):
    ah, al = split(a)
    return dot(ah, bh) + (dot(ah, bl) + dot(al, bh))


def put_halves(total, mine, other):
    same = lax.axis_index("xl") == lax.axis_index("xh")
    near, far = total[:, :128], total[:, 128:]
    mine[...] = jnp.where(same, near, far)
    other[...] = jnp.where(same, far, near)


def pack_kernel(offsets, *refs):
    n = len(offsets)
    near, far = refs[:n], refs[n : 2 * n]
    hi, lo, give = refs[2 * n :]
    y = lax.axis_index("y")
    c = lax.axis_index("c")
    for k, off in enumerate(offsets):
        first = 3 * lax.rem(y + (off + NY), NY)
        for t in range(3):
            rows = slice(t * 128, (t + 1) * 128)
            unit = jnp.concatenate([near[k][rows, :], far[k][rows, :]], axis=1)
            hi[first + t], lo[first + t] = split(unit)

            @pl.when(lax.rem(first + t, 2) != c)
            def _():
                give[(first + t) // 2] = unit


def pack(offsets, near, far):
    rows, cols = near[0].shape
    args = near + far
    half = jax.ShapeDtypeStruct((2 * NZ, 128, 2 * cols), BF16)
    return pl.pallas_call(
        functools.partial(pack_kernel, tuple(offsets)),
        out_shape=(half, half, jax.ShapeDtypeStruct((NZ, 128, 2 * cols), F32)),
        in_specs=[VM] * len(args),
        out_specs=(VM,) * 3,
        compiler_params=PARAMS,
    )(*args)


def rows_kernel(hi, lo, took, rows_hi, rows_lo):
    c = lax.axis_index("c")
    for z in range(NZ):
        rows_hi[z, :, :256] = hi[2 * z + c]
        rows_lo[z, :, :256] = lo[2 * z + c]
        rows_hi[z, :, 256:], rows_lo[z, :, 256:] = split(took[z])


def phase_rows(hi, lo, took):
    units, depth, cols = took.shape
    half = jax.ShapeDtypeStruct((units, depth, 2 * cols), BF16)
    return pl.pallas_call(
        rows_kernel,
        out_shape=(half, half),
        in_specs=[VM] * 3,
        out_specs=(VM, VM),
        compiler_params=PARAMS,
    )(hi, lo, took)


def first_kernel(left, hi, lo, mine, other, held, sems):
    parts, per = held.shape[:2]
    copies = [
        pltpu.make_async_copy(left.at[pl.ds(per * p, per)], held.at[p], sems.at[p]) for p in range(parts)
    ]
    for copy in copies:
        copy.start()
    for copy in copies:
        copy.wait()
    acc = None
    for z in range(NZ):
        u = 2 * z
        p, k = divmod(u, per)
        a = jnp.concatenate([held[p, k], held[p, k + 1]], axis=1)
        bh = jnp.concatenate([hi[u], hi[u + 1]], axis=0)
        bl = jnp.concatenate([lo[u], lo[u + 1]], axis=0)
        term = split_dot(a, bh, bl)
        acc = term if acc is None else acc + term
    put_halves(acc, mine, other)


def first_product(left, hi, lo):
    units, rows, cols = left.shape
    parts = 6
    block = jax.ShapeDtypeStruct((rows, cols), F32)
    return pl.pallas_call(
        first_kernel,
        out_shape=(block, block),
        in_specs=[HB, VM, VM],
        out_specs=(VM, VM),
        scratch_shapes=[
            pltpu.VMEM((parts, units // parts, rows, cols), F32),
            pltpu.SemaphoreType.DMA((parts,)),
        ],
        compiler_params=WIDE,
        cost_estimate=pl.CostEstimate(
            flops=NZ * 3 * 2 * rows * 2 * cols * 2 * cols, bytes_accessed=0, transcendentals=0
        ),
    )(left, hi, lo)


def second_kernel(offsets, has_acc, last, hi, lo, *refs):
    n = len(offsets)
    acc = refs[n][...] if has_acc else None
    outs = refs[n + has_acc :]
    z = lax.axis_index("z")
    at = [lax.rem(z + (off + NZ), NZ) for off in offsets]
    for k in range(0, n, 2):
        pair = range(k, min(k + 2, n))
        a = jnp.concatenate([refs[i][...] for i in pair], axis=1)
        bh = jnp.concatenate([hi[at[i]] for i in pair], axis=0)
        bl = jnp.concatenate([lo[at[i]] for i in pair], axis=0)
        term = split_dot(a, bh, bl)
        acc = term if acc is None else acc + term
    if last:
        outs[0][...] = acc[:, :256]
        outs[1][...] = acc[:, 256:]
    else:
        outs[0][...] = acc


def second_product(operand, blocks, acc=None, last=False):
    offsets = tuple(off for off, _ in blocks)
    rows, cols = blocks[0][1].shape
    args = list(operand) + [x for _, x in blocks] + ([] if acc is None else [acc])
    if last:
        shapes = (jax.ShapeDtypeStruct((rows, 2 * cols), F32),) * 2
    else:
        shapes = jax.ShapeDtypeStruct((rows, 4 * cols), F32)
    return pl.pallas_call(
        functools.partial(second_kernel, offsets, acc is not None, last),
        out_shape=shapes,
        in_specs=[VM] * len(args),
        out_specs=(VM, VM) if last else VM,
        compiler_params=PARAMS,
        cost_estimate=pl.CostEstimate(
            flops=len(offsets) * 3 * 2 * rows * cols * 4 * cols, bytes_accessed=0, transcendentals=0
        ),
    )(*args)


def join_kernel(hi, lo, own, both, last, mine, other):
    u = 2 * lax.rem(lax.axis_index("z") + NZ // 2, NZ)
    a = jnp.concatenate([last[0], last[1]], axis=1)
    bh = jnp.concatenate([hi[u], hi[u + 1]], axis=0)
    bl = jnp.concatenate([lo[u], lo[u + 1]], axis=0)
    total = own[...] + both[1 - lax.axis_index("c")] + split_dot(a, bh, bl)
    put_halves(total, mine, other)


def join(hi, lo, own, give, last):
    both = lax.all_gather(give, "c", axis=0)
    block = jax.ShapeDtypeStruct(last.shape, F32)
    args = (hi, lo, own, both, lax.all_gather(last, "c", axis=0))
    return pl.pallas_call(
        join_kernel,
        out_shape=(block, block),
        in_specs=[VM] * len(args),
        out_specs=(VM, VM),
        compiler_params=PARAMS,
    )(*args)


def filter_kernel(final, kept, mine, pair, *refs):
    other = 1 - lax.axis_index("xl")
    lane = lax.broadcasted_iota(jnp.int32, (BS, 2 * BS), 1)
    for i in range(kept.shape[1]):
        strip = slice(i * BS, (i + 1) * BS)
        filt = jnp.where(lane < BS, kept[0, i], kept[1, i]).astype(F32)
        total = filt * (mine[strip, :] + pair[other, strip, :])
        if final:
            square = refs[0][strip, :]
            refs[1][strip, :] = square
            refs[2][strip, :] = 3.0 * square - 2.0 * total
        else:
            refs[0][strip, :] = total


def filtered(kept, halves, square=None):
    mine, other = halves
    final = square is not None
    pair = lax.all_gather(other, "xl", axis=0)
    args = [kept, mine, pair] + ([square] if final else [])
    block = jax.ShapeDtypeStruct(mine.shape, F32)
    return pl.pallas_call(
        functools.partial(filter_kernel, final),
        out_shape=(block, block) if final else block,
        in_specs=[SM] + [VM] * (len(args) - 1),
        out_specs=(VM, VM) if final else VM,
        compiler_params=PARAMS,
    )(*args)


def shift(x, axis, step):
    n = SIZES[AXES.index(axis)]
    return lax.ppermute(x, axis, [(i, (i + step) % n) for i in range(n)])


def together(*xs):
    return lax.optimization_barrier(xs)


def chain(x, axis, step, count):
    out = []
    for _ in range(count):
        x = shift(x, axis, step)
        out.append(x)
    return out


def body(density, atom_sizes, pattern, kept):
    pattern = pattern.T
    masked = pl.pallas_call(
        mask_kernel,
        out_shape=jax.ShapeDtypeStruct(density.shape, F32),
        in_specs=[HB] * 3,
        out_specs=VM,
        scratch_shapes=[
            pltpu.SMEM(atom_sizes.shape, jnp.int32),
            pltpu.SMEM(pattern.shape, jnp.int32),
            pltpu.VMEM(density.shape, F32),
            pltpu.SemaphoreType.DMA((3,)),
        ],
        compiler_params=WHOLE,
    )(atom_sizes, pattern, density)

    left = lax.all_gather(masked, ("z", "c"), axis=0)

    near = lax.ppermute(masked, ("xh", "xl"), [(0, 0), (1, 2), (2, 1), (3, 3)])
    far = lax.ppermute(masked, ("xh", "xl"), [(1, 0), (2, 3), (0, 2), (3, 1)])
    near_up, near_down = chain(near, "y", 1, 4), chain(near, "y", -1, 3)
    far_up, far_down = chain(far, "y", 1, 3), chain(far, "y", -1, 4)
    offsets = [0, -1, 1, -2, 2, -3, 3, 4]
    near = [near] + [x for pair in zip(near_up, near_down) for x in pair] + [near_up[3]]
    far = [far] + [x for pair in zip(far_up, far_down) for x in pair] + [far_down[3]]
    hi, lo, give = pack(offsets, near, far)
    took = shift(give, "c", 1)
    mine, other, took = together(*first_product(left, hi, lo), took)
    square = filtered(kept.T, (mine, other))

    operand = phase_rows(hi, lo, took)
    up, down = chain(square, "z", 1, 6), chain(square, "z", -1, 5)
    blocks = [(0, square)]
    for s in range(5):
        blocks += [(-s - 1, up[s]), (s + 1, down[s])]
    acc = second_product(operand, blocks[:4])
    acc = second_product(operand, blocks[4:8], acc)
    halves = join(hi, lo, *second_product(operand, blocks[8:11], acc, last=True), up[5])
    return filtered(kept.T, halves, square)


def solution(mesh):
    fine = Mesh(mesh.devices.reshape(SIZES), AXES)
    placed = (P(ROW, COL), P(), P(ROW, COL), P(ROW, COL))
    return jax.shard_map(
        body,
        mesh=fine,
        in_specs=placed,
        out_specs=(P(ROW, COL), P(ROW, COL)),
        check_vma=False,
    )
```
